32 devices in a mesh: seg: 8 (over z, core), cfg: 4 (over y, x).
Axes of the slice: x: 2, y: 2, z: 4, core: 2. Of those that a mesh axis runs over, the one named last changes fastest.
Arguments:
- node_feats: bfloat16 [128, 2048, 256], P('cfg', 'seg'), may hold values from -6 to 6
- adjacency: int32 [2048, 288], P('seg'), may hold values 0 or 1
- halo_rows: int32 [8, 2, 16], P('seg'), may hold values from 0 to 255
- node_graph: int32 [2048], P('seg'), may hold values from 0 to 3, never falling along the last dimension, each value on 1 to 1536 neighbouring positions
- layer_weights: bfloat16 [3, 256, 256], replicated, may hold values from -0.375 to 0.375
- bilinear: bfloat16 [256, 256], replicated, may hold values from -0.0234375 to 0.0234375
- partners: int32 [4, 128, 64], P(None, 'cfg'), may hold values from 0 to 127
- ranking: int32 [4, 128], replicated, may hold values from 0 to 127, each once within a row
Outputs:
- embeddings: bfloat16 [4, 128, 256], P(None, 'cfg')
- weight_grad: float32 [256, 256], replicated
- hinge_loss: float32 [], replicated
The draws below stay inside these ranges and needn't reach their ends.
Inputs may be any that keep to these rules, and one draw needn't show every extreme that they name: `adjacency`: columns are, in order, the 16 rows read from the previous segment, the segment's own 256 nodes, the 16 rows read from the next segment. halo_rows[s, 0, :] are rows of segment s read by segment s-1, halo_rows[s, 1, :] rows read by segment s+1; repeats may occur. `node_graph`: never falls along the nodes; each graph has 1 to 1536 nodes, one exactly that many. `ranking`: each row is a permutation.
All inputs are finite; a program needn't handle non-finite values. No bound on the sum of `adjacency` on one device may be relied on, other than what follows from the above.
Results may differ from the reference program's by a relative error of at most 0.0034.
Values may be sent and summed in bfloat16 or wider, within the bound.
A program may use at most 64 MiB of HBM per device.

```python
import math
import jax
import jax.numpy as jnp
import numpy as np
from jax import lax

F = 256
N_DEV = 256
H = 16
L = 3
C = 128
P_SIZE = 64
G = 4
SEGS = 8
NODES = 2048


def place_ends(entries, own_key, least, top_value):
    longest = entries.shape.index(max(entries.shape))
    spots = []
    for shift in (0, 1):
        where = [jax.random.randint(jax.random.fold_in(own_key, axis), (), 0, length) for axis, length in enumerate(entries.shape)]
        where[longest] = (where[longest] + shift) % entries.shape[longest]
        spots.append(tuple(where))
    return entries.at[spots[0]].set(least).at[spots[1]].set(top_value)


def with_spikes(result, key, source, target, blocks, factor):
    def block_of(dim):
        return (jnp.arange(result.shape[dim]) // (result.shape[dim] // blocks)).reshape((-1,) + (1,) * (result.ndim - 1 - dim))

    first = jax.random.permutation(key, blocks)[block_of(target)]
    second = (block_of(target) + blocks // 2) % blocks
    return jnp.where((block_of(source) == first) | (block_of(source) == second), factor * result, result)


def shard_levels(key, dims, pieces, smallest, largest):
    gain, own = 1.0, jax.random.fold_in(key, 6)
    for axis_at, parts in pieces:
        heights = jnp.exp(jax.random.uniform(jax.random.fold_in(own, axis_at), (parts,), jnp.float32, smallest / len(pieces), largest / len(pieces)))
        gain = gain * jnp.repeat(heights, dims[axis_at] // parts).reshape([-1 if axis == axis_at else 1 for axis in range(len(dims))])
    return gain


def profile(number_of, total, limit, lean):
    loads = [(1 << 20) // math.isqrt(rank ** lean) + 1 for rank in range(2, number_of + 1)]
    rest, counts = total - limit - (number_of - 1), [1] * (number_of - 1)
    while rest > 0:
        free = [i for i in range(number_of - 1) if counts[i] < limit]
        mass, budget = sum([loads[i] for i in free]), rest
        for i in free:
            addition = min(limit - counts[i], max(1, budget * loads[i] // mass), rest)
            counts[i] = counts[i] + addition
            rest = rest - addition
    return np.array([limit] + counts)


def uneven_parts(own_key, amount, total, reach, skew):
    if amount == 2:
        one = jax.random.randint(own_key, (), max(1, total - reach), min(reach, total - 1) + 1)
        return jnp.stack([one, total - one])
    lengths = jnp.asarray(profile(amount, total, reach, skew), jnp.int32)
    couples = (amount - 1) // 2
    source_of, receiver = lengths[1:1 + 2 * couples:2], lengths[2:2 + 2 * couples:2]
    room = jnp.minimum(source_of - 1, reach - receiver)
    moved = jax.random.randint(jax.random.fold_in(own_key, 1), (couples,), 0, 1 << 20) % (room + 1)
    lengths = lengths.at[1:1 + 2 * couples:2].set(source_of - moved).at[2:2 + 2 * couples:2].set(receiver + moved)
    return lengths[jax.random.permutation(jax.random.fold_in(own_key, 2), amount)]


def gaussian(rng, shape, width, most, split=(), kind=jnp.bfloat16):
    drawn = width * jax.random.normal(rng, shape, jnp.float32)
    if split:
        drawn = drawn * shard_levels(rng, shape, split, -0.22, 0.18)
    return jnp.clip(drawn, -most, most).astype(kind)


def bell_draw_with(stream_key, dims, width, most, cuts, heavy, kind=jnp.bfloat16):
    values = width * jax.random.normal(stream_key, dims, jnp.float32)
    if cuts:
        values = values * shard_levels(stream_key, dims, cuts, -0.22, 0.18)
    return jnp.clip(with_spikes(values, jax.random.fold_in(stream_key, 3), *heavy), -most, most).astype(kind)


def setup_inputs(seed: int = 0) -> dict:
    key_list = jax.random.split(jax.random.key(seed), 9)
    node_feats = bell_draw_with(key_list[0], (C, NODES, F), 1.0, 6.0, ((0, 4), (1, 8)), (1, 0, 8, 2.0))
    adjacency = place_ends((jax.random.randint(key_list[1], (NODES, N_DEV + 2 * H), 0, 8) < 1).astype(jnp.int32), jax.random.fold_in(key_list[1], 1), 0, 1)
    halo_rows = place_ends(jax.random.randint(key_list[2], (SEGS, 2, H), 0, N_DEV), jax.random.fold_in(key_list[2], 1), 0, N_DEV - 1).astype(jnp.int32)
    node_graph = jnp.searchsorted(jnp.cumsum(uneven_parts(key_list[3], G, NODES, 3 * NODES // 4, 0)), jnp.arange(NODES), side="right").astype(jnp.int32)
    layer_weights = gaussian(key_list[4], (L, F, F), F ** -0.5, 0.375)
    bilinear = gaussian(key_list[5], (F, F), (F * F) ** -0.5, 0.0234375)
    partners = place_ends(jax.random.randint(key_list[6], (G, C, P_SIZE), 0, C), jax.random.fold_in(key_list[6], 1), 0, C - 1).astype(jnp.int32)
    ranking = jax.vmap(lambda own: jax.random.permutation(own, C))(jax.random.split(key_list[7], G)).reshape((G, C)).astype(jnp.int32)
    return dict(node_feats=node_feats, adjacency=adjacency, halo_rows=halo_rows, node_graph=node_graph, layer_weights=layer_weights, bilinear=bilinear, partners=partners, ranking=ranking)


high_precision_mode = lax.Precision.HIGHEST
eps = 1e-06

def rms_scale(values):
    return values * lax.rsqrt(lax.optimization_barrier(jnp.mean(values * values, axis=-1, keepdims=True)) + eps)

def graph_block(cfg_block, adjacency, halo_rows, node_graph, layer_weights):
    block_size = cfg_block.shape[0]
    seg_count = halo_rows.shape[0]
    adj_float = adjacency.reshape(seg_count, N_DEV, N_DEV + 2 * H).astype(jnp.float32)
    degree = lax.optimization_barrier(jnp.sum(adj_float, axis=-1))
    hidden = cfg_block.reshape(block_size, seg_count, N_DEV, F)
    pick_rows = jax.vmap(lambda table, picks: table[:, picks, :], in_axes=(1, 0), out_axes=1)
    for layer_idx in range(L):
        to_prev = pick_rows(hidden, halo_rows[:, 0, :])
        forward_halo = pick_rows(hidden, halo_rows[:, 1, :])
        empty_rim = jnp.zeros_like(to_prev[:, :1])
        prev_rim = jnp.concatenate([empty_rim, forward_halo[:, :-1]], axis=1)
        next_rim = jnp.concatenate([to_prev[:, 1:], empty_rim], axis=1)
        extended = jnp.concatenate([prev_rim, hidden, next_rim], axis=2)
        summed = jnp.einsum('snm,bsmf->bsnf', adj_float, extended.astype(jnp.float32), precision=high_precision_mode)
        summed = summed + hidden.astype(jnp.float32)
        mixed = summed / (1.0 + degree)[None, :, :, None]
        normed = rms_scale(mixed).astype(jnp.bfloat16)
        branch = jnp.einsum('bsnf,fg->bsng', normed.astype(jnp.float32), layer_weights[layer_idx].astype(jnp.float32), precision=high_precision_mode)
        hidden = (hidden.astype(jnp.float32) + jax.nn.silu(branch)).astype(jnp.bfloat16)
    flattened = hidden.reshape(block_size, seg_count * N_DEV, F)
    onehot = (node_graph[None, :] == jnp.arange(G, dtype=jnp.int32)[:, None]).astype(jnp.float32)
    return jnp.einsum('gn,bnf->gbf', onehot, flattened.astype(jnp.float32), precision=high_precision_mode)

def reference(node_feats, adjacency, halo_rows, node_graph, layer_weights, bilinear, partners, ranking):
    block_size = 8
    blocks = node_feats.reshape(C // block_size, block_size, NODES, F)
    pooled = lax.map(lambda cfg_block: graph_block(cfg_block, adjacency, halo_rows, node_graph, layer_weights), blocks)
    pooled = jnp.transpose(pooled, (1, 0, 2, 3)).reshape(G, C, F)
    embedding = rms_scale(pooled).astype(jnp.bfloat16)
    embed_f32 = embedding.astype(jnp.float32)
    projected_rows = jnp.einsum('gcf,fh->gch', embed_f32, bilinear.astype(jnp.float32), precision=high_precision_mode)
    partner_embedding = jax.vmap(lambda table, picks: table[picks])(embed_f32, partners)
    config_scores = jnp.einsum('noz,noxz->nox', projected_rows, partner_embedding, precision=high_precision_mode)
    their_rank = jax.vmap(lambda table, picks: table[picks])(ranking, partners)
    pairwise_direction = jnp.sign((their_rank - ranking[:, :, None]).astype(jnp.float32))
    margin = 1.0 - pairwise_direction * config_scores
    pair_loss = jnp.sum(jax.nn.softplus(margin)) / (G * C * P_SIZE)
    pairwise_factor = -pairwise_direction * jax.nn.sigmoid(margin) / (G * P_SIZE)
    carry_over_rows = jnp.einsum('tve,tvef->tvf', pairwise_factor, partner_embedding, precision=high_precision_mode)
    weight_grad = jnp.einsum('gcf,gch->fh', embed_f32, carry_over_rows, precision=high_precision_mode)
    return (embedding, weight_grad, pair_loss)
```

```python
import functools

import jax
import jax.numpy as jnp
from jax import lax
from jax.experimental import pallas as pl
from jax.experimental.pallas import tpu as pltpu
from jax.sharding import PartitionSpec as P

P_SIZE = 64
G = 4
eps = 1e-06
MESH = pl.DeviceIdType.MESH
f32, bf16 = jnp.float32, jnp.bfloat16


def dot(a, b):
    return jnp.dot(a, b, preferred_element_type=f32)


def split3(values):
    high = values.astype(bf16)
    rest = values - high.astype(f32)
    middle = rest.astype(bf16)
    low = (rest - middle.astype(f32)).astype(bf16)
    return high, middle, low


def each(count, fn):
    lax.fori_loop(0, count, lambda i, c: (fn(i), c)[1], 0)


def column(row, size):
    rows = lax.broadcasted_iota(jnp.int32, (size, size), 0)
    lanes = lax.broadcasted_iota(jnp.int32, (size, size), 1)
    return jnp.sum(jnp.where(rows == lanes, jnp.broadcast_to(row, (size, size)), 0.0), axis=1, keepdims=True)


def kernel(
    sizes,
    feats, adjacency, halo_rows, node_graph, weights, bilinear, partners, ranking,
    emb_out, grad_out, loss_out,
    ext0, ext1, ext2, outbox, pooled, parts, emb_all, cnt_all, sgn, adj_mat, pick, member, half_w, eps_col,
    in_sem, halo_send, halo_recv, pool_send, pool_recv, seg_send, seg_recv, cfg_send, cfg_recv, cnt_send, cnt_recv,
):
    S, Q, configs, nodes, feat, rim, layers, unroll, own_rows, owners = sizes
    exts = (ext0, ext1, ext2)
    chunks = configs // unroll
    total = Q * configs
    seg, cfg = lax.axis_index("seg"), lax.axis_index("cfg")

    barrier = pltpu.get_barrier_semaphore()

    def greet(axis, me, count):
        def one(k):
            pl.semaphore_signal(barrier, inc=1, device_id={axis: lax.rem(me + k + 1, count)}, device_id_type=MESH)
        each(count - 1, one)

    greet("seg", seg, S)
    greet("cfg", cfg, Q)

    def load(i):
        return pltpu.make_async_copy(
            feats.at[pl.ds(i * unroll, unroll)],
            ext0.at[pl.ds(i * unroll, unroll), pl.ds(rim, nodes)],
            in_sem.at[i],
        )

    each(chunks, lambda i: load(i).start())

    adj = adjacency[...].astype(f32)
    degree = jnp.sum(adj, axis=1, keepdims=True)
    rows = lax.broadcasted_iota(jnp.int32, adj.shape, 0)
    lanes = lax.broadcasted_iota(jnp.int32, adj.shape, 1)
    adj_mat[...] = (adj + jnp.where(lanes == rows + rim, 1.0, 0.0)).astype(bf16)
    eps_col[...] = eps * (1.0 + degree) * (1.0 + degree)
    half_w[...] = (weights[...].astype(f32) * 0.5).astype(bf16)
    node_ids = lax.broadcasted_iota(jnp.int32, (rim, nodes), 1).astype(f32)
    for side in range(2):
        wanted = column(halo_rows[side : side + 1, :].astype(f32), rim)
        pick[side * rim : (side + 1) * rim, :] = jnp.where(node_ids == wanted, 1.0, 0.0).astype(bf16)
    graph_ids = lax.broadcasted_iota(jnp.int32, (16, nodes), 0)
    member[...] = jnp.where(graph_ids == jnp.broadcast_to(node_graph[...], (16, nodes)), 1.0, 0.0).astype(bf16)

    @pl.when(seg == 0)
    def _():
        for ext in exts:
            ext[:, 0:rim, :] = jnp.zeros((configs, rim, feat), bf16)

    @pl.when(seg == S - 1)
    def _():
        for ext in exts:
            ext[:, rim + nodes : 2 * rim + nodes, :] = jnp.zeros((configs, rim, feat), bf16)

    pl.semaphore_wait(barrier, S + Q - 2)

    def halo_copy(l, i, side):
        batch = pl.ds(i * unroll, unroll)
        return pltpu.make_async_remote_copy(
            src_ref=outbox.at[l, batch, pl.ds(side * rim, rim)],
            dst_ref=exts[l].at[batch, pl.ds(0 if side else rim + nodes, rim)],
            send_sem=halo_send.at[l, side, i],
            recv_sem=halo_recv.at[l, side, i],
            device_id={"seg": seg + 1 if side else seg - 1},
            device_id_type=MESH,
        )

    def halo_each(l, i, sends, act):
        up, down = seg < S - 1, seg > 0

        @pl.when(down if sends else up)
        def _():
            act(halo_copy(l, i, 0))

        @pl.when(up if sends else down)
        def _():
            act(halo_copy(l, i, 1))

    def first(i):
        load(i).wait()
        for u in range(unroll):
            c = i * unroll + u
            outbox[0, c] = dot(pick[...], ext0[c, rim : rim + nodes, :]).astype(bf16)
        halo_each(0, i, True, lambda copy: copy.start())

    each(chunks, first)

    def layer(l, i):
        halo_each(l, i, False, lambda copy: copy.wait_recv())
        for u in range(unroll):
            c = i * unroll + u
            summed = dot(adj_mat[...], exts[l][c])
            square = jnp.sum(summed * summed, axis=1, keepdims=True) * (1.0 / feat)
            normed = (summed * lax.rsqrt(square + eps_col[...])).astype(bf16)
            half = dot(normed, half_w[l])
            before = exts[l][c, rim : rim + nodes, :].astype(f32)
            hidden = (before + (half + half * jnp.tanh(half))).astype(bf16)
            if l < layers - 1:
                exts[l + 1][c, rim : rim + nodes, :] = hidden
                outbox[l + 1, c] = dot(pick[...], hidden).astype(bf16)
            else:
                sums = dot(member[...], hidden)
                for g in range(G):
                    pooled[pl.ds(g * configs + c, 1), :] = sums[g : g + 1, :]
        if l < layers - 1:
            halo_each(l + 1, i, True, lambda copy: copy.start())

    for l in range(layers - 1):
        each(chunks, functools.partial(layer, l))

    def pool_copy(source, o):
        return pltpu.make_async_remote_copy(
            src_ref=pooled.at[pl.ds(o * own_rows, own_rows)],
            dst_ref=parts.at[source],
            send_sem=pool_send.at[o],
            recv_sem=pool_recv.at[source],
            device_id={"seg": o},
            device_id_type=MESH,
        )

    groups = max(1, configs // own_rows)
    per_group = chunks // groups

    def last_group(p):
        each(per_group, lambda j: layer(layers - 1, p * per_group + j))

        def send(k):
            o = k * groups + p

            @pl.when(o != seg)
            def _():
                pool_copy(seg, o).start()

        each(owners // groups, send)

    each(groups, last_group)

    block = 16 if (G * configs) % 16 == 0 else 8

    def count(r):
        where = pl.ds(pl.multiple_of(r * block, block), block)
        chosen = partners[where, :]
        ids = lax.broadcasted_iota(jnp.int32, (block, total), 1)
        found = jnp.zeros((block, total), f32)
        for k in range(P_SIZE):
            found = found + jnp.where(chosen[:, k : k + 1] == ids, 1.0, 0.0)
        cnt_all[cfg, where, :] = found.astype(bf16)

    each(G * configs // block, count)

    def cnt_copy(d):
        return pltpu.make_async_remote_copy(
            src_ref=cnt_all.at[cfg],
            dst_ref=cnt_all.at[cfg],
            send_sem=cnt_send.at[d],
            recv_sem=cnt_recv.at[d],
            device_id={"cfg": lax.rem(cfg + d + 1, Q)},
            device_id_type=MESH,
        )

    each(Q - 1, lambda d: cnt_copy(d).start())

    for g in range(G):
        theirs = jnp.broadcast_to(ranking[g : g + 1, :].astype(f32), (total, total))
        ahead = theirs - column(ranking[g : g + 1, :].astype(f32), total)
        sgn[g] = jnp.where(ahead > 0.0, 1.0, jnp.where(ahead < 0.0, -1.0, 0.0))

    def emb_block(q, o):
        return emb_all.at[q, pl.ds(o * own_rows, own_rows)]

    def seg_copy(k, o):
        return pltpu.make_async_remote_copy(
            src_ref=emb_block(cfg, o),
            dst_ref=emb_block(cfg, o),
            send_sem=seg_send.at[k],
            recv_sem=seg_recv.at[o],
            device_id={"seg": lax.rem(seg + k + 1, S)},
            device_id_type=MESH,
        )

    def cfg_copy(d, q, o):
        return pltpu.make_async_remote_copy(
            src_ref=emb_block(q, o),
            dst_ref=emb_block(q, o),
            send_sem=cfg_send.at[d, o],
            recv_sem=cfg_recv.at[d, o],
            device_id={"cfg": lax.rem(cfg + d + 1, Q)},
            device_id_type=MESH,
        )

    @pl.when(seg < owners)
    def _():
        parts[seg] = pooled[pl.ds(pl.multiple_of(seg * own_rows, own_rows), own_rows), :]

        def arrive(k):
            pool_copy(lax.rem(seg + k + 1, S), seg).wait_recv()

        each(S - 1, arrive)
        summed = parts[0]
        for s in range(1, S):
            summed = summed + parts[s]
        square = jnp.sum(summed * summed, axis=1, keepdims=True) * (1.0 / feat)
        mine = pl.ds(pl.multiple_of(seg * own_rows, own_rows), own_rows)
        emb_all[cfg, mine, :] = (summed * lax.rsqrt(square + eps)).astype(bf16)
        each(S - 1, lambda k: seg_copy(k, seg).start())

    def forward(k):
        o = lax.rem(seg + k, owners)

        @pl.when(o != seg)
        def _():
            seg_copy(0, o).wait_recv()

        each(Q - 1, lambda d: cfg_copy(d, cfg, o).start())

    each(owners, forward)

    for l in range(layers):
        each(chunks, lambda i: halo_each(l, i, True, lambda copy: copy.wait_send()))

    def sent(o):
        @pl.when(o != seg)
        def _():
            pool_copy(seg, o).wait_send()

    each(owners, sent)

    @pl.when(seg < owners)
    def _():
        each(S - 1, lambda k: seg_copy(k, seg).wait_send())

    each(Q - 1, lambda d: cnt_copy(d).wait())

    def arrived(d):
        source = lax.rem(cfg + Q - d - 1, Q)
        each(owners, lambda o: cfg_copy(d, source, o).wait_recv())

    each(Q - 1, arrived)
    emb_out[...] = emb_all[cfg]

    def of_graph(ref, g):
        if configs % 16 == 0:
            rows = ref[:, g * configs : (g + 1) * configs, :]
        else:
            rows = ref[...].astype(f32)[:, g * configs : (g + 1) * configs, :]
        return rows.reshape(total, rows.shape[2]).astype(bf16)

    grad = jnp.zeros((feat, feat), f32)
    loss = jnp.zeros((1, 1), f32)
    for g in range(G):
        emb = of_graph(emb_all, g)
        often = of_graph(cnt_all, g).astype(f32)
        emb_t = emb.astype(f32).T.astype(bf16)
        projected = dot(emb, bilinear[...])
        stacked = dot(jnp.concatenate(split3(projected), axis=0), emb_t)
        scores = stacked[:total] + stacked[total : 2 * total] + stacked[2 * total :]
        sign = sgn[g]
        margin = 1.0 - sign * scores
        decay = jnp.exp(-jnp.abs(margin))
        soft = jnp.maximum(margin, 0.0) + jnp.log1p(decay)
        sigmoid = jnp.where(margin >= 0.0, 1.0, decay) / (1.0 + decay)
        loss = loss + jnp.sum(often * soft, axis=(0, 1), keepdims=True)
        coef = often * (-sign) * sigmoid * (1.0 / (G * P_SIZE))
        stacked = dot(jnp.concatenate(split3(coef), axis=0), emb)
        carried = stacked[:total] + stacked[total : 2 * total] + stacked[2 * total :]
        high, middle, low = split3(carried)
        grad = grad + (dot(emb_t, high) + dot(emb_t, middle) + dot(emb_t, low))
    grad_out[...] = grad
    loss_out[...] = loss * (1.0 / (G * total * P_SIZE))

    def cfg_sent(d):
        each(owners, lambda o: cfg_copy(d, cfg, o).wait_send())

    each(Q - 1, cfg_sent)


def on_device(S, Q, node_feats, adjacency, halo_rows, node_graph, layer_weights, bilinear, partners, ranking):
    configs, nodes, feat = node_feats.shape
    rim, layers = halo_rows.shape[2], layer_weights.shape[0]
    unroll = 4
    chunks = configs // unroll
    own_rows = max(16, G * configs // S)
    owners = G * configs // own_rows
    total = Q * configs
    wide = nodes + 2 * rim
    sizes = (S, Q, configs, nodes, feat, rim, layers, unroll, own_rows, owners)
    vmem = pl.BlockSpec(memory_space=pltpu.VMEM)
    dma = pltpu.SemaphoreType.DMA
    emb, grad, loss = pl.pallas_call(
        functools.partial(kernel, sizes),
        out_shape=(
            jax.ShapeDtypeStruct((G * configs, feat), bf16),
            jax.ShapeDtypeStruct((feat, feat), f32),
            jax.ShapeDtypeStruct((1, 1), f32),
        ),
        in_specs=[pl.BlockSpec(memory_space=pl.ANY)] + [vmem] * 7,
        out_specs=(vmem, vmem, vmem),
        scratch_shapes=[pltpu.VMEM((configs, wide, feat), bf16)] * 3
        + [
            pltpu.VMEM((layers, configs, 2 * rim, feat), bf16),
            pltpu.VMEM((G * configs, feat), f32),
            pltpu.VMEM((S, own_rows, feat), f32),
            pltpu.VMEM((Q, G * configs, feat), bf16),
            pltpu.VMEM((Q, G * configs, total), bf16),
            pltpu.VMEM((G, total, total), f32),
            pltpu.VMEM((nodes, wide), bf16),
            pltpu.VMEM((2 * rim, nodes), bf16),
            pltpu.VMEM((16, nodes), bf16),
            pltpu.VMEM((layers, feat, feat), bf16),
            pltpu.VMEM((nodes, 1), f32),
            dma((chunks,)),
            dma((layers, 2, chunks)),
            dma((layers, 2, chunks)),
            dma((owners,)),
            dma((S,)),
            dma((S - 1,)),
            dma((owners,)),
            dma((Q - 1, owners)),
            dma((Q - 1, owners)),
            dma((Q - 1,)),
            dma((Q - 1,)),
        ],
        compiler_params=pltpu.CompilerParams(
            collective_id=0, has_side_effects=True, vmem_limit_bytes=48 * 1024 * 1024
        ),
    )(
        node_feats,
        adjacency,
        halo_rows.reshape(2, rim),
        node_graph.reshape(1, nodes),
        layer_weights,
        bilinear,
        partners.reshape(G * configs, partners.shape[2]),
        ranking,
    )
    return emb.reshape(G, configs, feat), grad, loss.reshape(())


def solution(mesh):
    placed = (
        P("cfg", "seg", None),
        P("seg", None),
        P("seg", None, None),
        P("seg"),
        P(),
        P(),
        P(None, "cfg", None),
        P(),
    )
    return jax.shard_map(
        functools.partial(on_device, mesh.shape["seg"], mesh.shape["cfg"]),
        mesh=mesh,
        in_specs=placed,
        out_specs=(P(None, "cfg", None), P(), P()),
        check_vma=False,
    )
```

```python
import functools

import jax
import jax.numpy as jnp
from jax import lax
from jax.experimental import pallas as pl
from jax.experimental.pallas import tpu as pltpu
from jax.sharding import PartitionSpec as P

P_SIZE = 64
G = 4
LANES = 128
eps = 1e-06
MESH = pl.DeviceIdType.MESH
f32, bf16 = jnp.float32, jnp.bfloat16


def dot(a, b):
    return jnp.dot(a, b, preferred_element_type=f32)


def split3(values):
    high = values.astype(bf16)
    rest = values - high.astype(f32)
    middle = rest.astype(bf16)
    low = (rest - middle.astype(f32)).astype(bf16)
    return high, middle, low


def each(count, fn):
    lax.fori_loop(0, count, lambda i, c: (fn(i), c)[1], 0)


def column(row, size):
    rows = lax.broadcasted_iota(jnp.int32, (size, size), 0)
    lanes = lax.broadcasted_iota(jnp.int32, (size, size), 1)
    return jnp.sum(jnp.where(rows == lanes, jnp.broadcast_to(row, (size, size)), 0.0), axis=1, keepdims=True)


def kernel(
    sizes,
    feats, *rest,
):
    compute(sizes, feats, rest[:7], *rest[7:])


def compute(
    sizes, feats, sources,
    emb_out, grad_out, loss_out,
    ext0, ext1, ext2, outbox, pooled, parts, emb_all, cnt_all, sgn, adj_mat, pick, member, half_w, eps_wide,
    adjacency, halo_rows, node_graph, weights, bilinear, partners, ranking, small_sem,
    in_sem, halo_send, halo_recv, pool_send, pool_recv, seg_send, seg_recv, cfg_send, cfg_recv, cnt_send, cnt_recv,
):
    S, Q, configs, nodes, feat, rim, layers, unroll, own_rows, owners = sizes
    exts = (ext0, ext1, ext2)
    chunks = configs // unroll
    total = Q * configs
    seg, cfg = lax.axis_index("seg"), lax.axis_index("cfg")

    barrier = pltpu.get_barrier_semaphore()

    def greet(axis, me, count):
        def one(k):
            pl.semaphore_signal(barrier, inc=1, device_id={axis: lax.rem(me + k + 1, count)}, device_id_type=MESH)
        each(count - 1, one)

    greet("seg", seg, S)
    greet("cfg", cfg, Q)

    copies = [
        pltpu.make_async_copy(source, target, small_sem.at[n])
        for n, (source, target) in enumerate(
            zip(sources, (adjacency, halo_rows, node_graph, weights, bilinear, partners, ranking))
        )
    ]
    for copy in copies:
        copy.start()

    def load(i):
        return pltpu.make_async_copy(
            feats.at[pl.ds(i * unroll, unroll)],
            ext0.at[pl.ds(i * unroll, unroll), pl.ds(rim, nodes)],
            in_sem.at[i],
        )

    each(chunks, lambda i: load(i).start())

    for copy in copies:
        copy.wait()
    wide = nodes + 2 * rim
    padded = -(-wide // LANES) * LANES
    turned = jnp.concatenate([adjacency[...].astype(f32), jnp.zeros((padded - wide, nodes), f32)], axis=0)
    adj = turned.T[:, :wide]
    degree = jnp.sum(adj, axis=1, keepdims=True)
    rows = lax.broadcasted_iota(jnp.int32, adj.shape, 0)
    lanes = lax.broadcasted_iota(jnp.int32, adj.shape, 1)
    adj_mat[...] = (adj + jnp.where(lanes == rows + rim, 1.0, 0.0)).astype(bf16)
    eps_wide[...] = jnp.broadcast_to(eps * (1.0 + degree) * (1.0 + degree), (nodes, LANES))
    half_w[...] = (weights[...].astype(f32) * 0.5).astype(bf16)
    node_ids = lax.broadcasted_iota(jnp.int32, (rim, nodes), 1).astype(f32)
    for side in range(2):
        wanted = column(halo_rows[side : side + 1, :].astype(f32), rim)
        pick[side * rim : (side + 1) * rim, :] = jnp.where(node_ids == wanted, 1.0, 0.0).astype(bf16)
    graph_ids = lax.broadcasted_iota(jnp.int32, (16, nodes), 0)
    member[...] = jnp.where(graph_ids == jnp.broadcast_to(node_graph[...], (16, nodes)), 1.0, 0.0).astype(bf16)

    @pl.when(seg == 0)
    def _():
        for ext in exts:
            ext[:, 0:rim, :] = jnp.zeros((configs, rim, feat), bf16)

    @pl.when(seg == S - 1)
    def _():
        for ext in exts:
            ext[:, rim + nodes : 2 * rim + nodes, :] = jnp.zeros((configs, rim, feat), bf16)

    pl.semaphore_wait(barrier, S + Q - 2)

    def halo_copy(l, i, side):
        batch = pl.ds(i * unroll, unroll)
        return pltpu.make_async_remote_copy(
            src_ref=outbox.at[l, batch, pl.ds(side * rim, rim)],
            dst_ref=exts[l].at[batch, pl.ds(0 if side else rim + nodes, rim)],
            send_sem=halo_send.at[l, side, i],
            recv_sem=halo_recv.at[l, side, i],
            device_id={"seg": seg + 1 if side else seg - 1},
            device_id_type=MESH,
        )

    def halo_each(l, i, sends, act):
        up, down = seg < S - 1, seg > 0

        @pl.when(down if sends else up)
        def _():
            act(halo_copy(l, i, 0))

        @pl.when(up if sends else down)
        def _():
            act(halo_copy(l, i, 1))

    def first(i):
        load(i).wait()
        ids = [i * unroll + u for u in range(unroll)]
        blocks = [ext0[c, rim : rim + nodes, :] for c in ids]
        picked = [dot(pick[...], block).astype(bf16) for block in blocks]
        for c, rows in zip(ids, picked):
            outbox[0, c] = rows
        halo_each(0, i, True, lambda copy: copy.start())

    each(chunks, first)

    def layer(l, i):
        halo_each(l, i, False, lambda copy: copy.wait_recv())
        ids = [i * unroll + u for u in range(unroll)]
        before = [exts[l][c] for c in ids]
        summed = [dot(adj_mat[...], block) for block in before]
        normed = []
        for values in summed:
            square = jnp.sum(values * values, axis=1, keepdims=True) * (1.0 / feat)
            scale = lax.rsqrt(jnp.broadcast_to(square, eps_wide.shape) + eps_wide[...])
            normed.append((values * jnp.tile(scale, (1, feat // LANES))).astype(bf16))
        halves = dot(jnp.concatenate(normed, axis=0), half_w[l])
        hidden = []
        for u in range(unroll):
            half = halves[u * nodes : (u + 1) * nodes]
            own = before[u][rim : rim + nodes].astype(f32)
            hidden.append((own + (half + half * jnp.tanh(half))).astype(bf16))
        if l < layers - 1:
            picked = [dot(pick[...], values).astype(bf16) for values in hidden]
            for c, values, rows in zip(ids, hidden, picked):
                exts[l + 1][c, rim : rim + nodes, :] = values
                outbox[l + 1, c] = rows
        else:
            sums = [dot(member[...], values) for values in hidden]
            for c, values in zip(ids, sums):
                for g in range(G):
                    pooled[pl.ds(g * configs + c, 1), :] = values[g : g + 1, :]
        if l < layers - 1:
            halo_each(l + 1, i, True, lambda copy: copy.start())

    for l in range(layers - 1):
        each(chunks, functools.partial(layer, l))

    def pool_copy(source, o):
        return pltpu.make_async_remote_copy(
            src_ref=pooled.at[pl.ds(o * own_rows, own_rows)],
            dst_ref=parts.at[source],
            send_sem=pool_send.at[o],
            recv_sem=pool_recv.at[source],
            device_id={"seg": o},
            device_id_type=MESH,
        )

    groups = max(1, configs // own_rows)
    per_group = chunks // groups

    def last_group(p):
        each(per_group, lambda j: layer(layers - 1, p * per_group + j))

        def send(k):
            o = k * groups + p

            @pl.when(o != seg)
            def _():
                pool_copy(seg, o).start()

        each(owners // groups, send)

    each(groups, last_group)

    block = 16 if (G * configs) % 16 == 0 else 8

    def count(r):
        where = pl.ds(pl.multiple_of(r * block, block), block)
        chosen = partners[where, :]
        ids = lax.broadcasted_iota(jnp.int32, (block, total), 1)
        found = jnp.zeros((block, total), f32)
        for k in range(P_SIZE):
            found = found + jnp.where(chosen[:, k : k + 1] == ids, 1.0, 0.0)
        cnt_all[cfg, where, :] = found.astype(bf16)

    each(G * configs // block, count)

    def cnt_copy(d):
        return pltpu.make_async_remote_copy(
            src_ref=cnt_all.at[cfg],
            dst_ref=cnt_all.at[cfg],
            send_sem=cnt_send.at[d],
            recv_sem=cnt_recv.at[d],
            device_id={"cfg": lax.rem(cfg + d + 1, Q)},
            device_id_type=MESH,
        )

    each(Q - 1, lambda d: cnt_copy(d).start())

    for g in range(G):
        theirs = jnp.broadcast_to(ranking[g : g + 1, :].astype(f32), (total, total))
        ahead = theirs - column(ranking[g : g + 1, :].astype(f32), total)
        sgn[g] = jnp.where(ahead > 0.0, 1.0, jnp.where(ahead < 0.0, -1.0, 0.0))

    def emb_block(q, o):
        return emb_all.at[q, pl.ds(o * own_rows, own_rows)]

    def seg_copy(k, o):
        return pltpu.make_async_remote_copy(
            src_ref=emb_block(cfg, o),
            dst_ref=emb_block(cfg, o),
            send_sem=seg_send.at[k],
            recv_sem=seg_recv.at[o],
            device_id={"seg": lax.rem(seg + k + 1, S)},
            device_id_type=MESH,
        )

    def cfg_copy(d, q, o):
        return pltpu.make_async_remote_copy(
            src_ref=emb_block(q, o),
            dst_ref=emb_block(q, o),
            send_sem=cfg_send.at[d, o],
            recv_sem=cfg_recv.at[d, o],
            device_id={"cfg": lax.rem(cfg + d + 1, Q)},
            device_id_type=MESH,
        )

    @pl.when(seg < owners)
    def _():
        parts[seg] = pooled[pl.ds(pl.multiple_of(seg * own_rows, own_rows), own_rows), :]

        def arrive(k):
            pool_copy(lax.rem(seg + k + 1, S), seg).wait_recv()

        each(S - 1, arrive)
        summed = parts[0]
        for s in range(1, S):
            summed = summed + parts[s]
        square = jnp.sum(summed * summed, axis=1, keepdims=True) * (1.0 / feat)
        mine = pl.ds(pl.multiple_of(seg * own_rows, own_rows), own_rows)
        emb_all[cfg, mine, :] = (summed * lax.rsqrt(square + eps)).astype(bf16)
        each(S - 1, lambda k: seg_copy(k, seg).start())

    def forward(k):
        o = lax.rem(seg + k, owners)

        @pl.when(o != seg)
        def _():
            seg_copy(0, o).wait_recv()

        each(Q - 1, lambda d: cfg_copy(d, cfg, o).start())

    each(owners, forward)

    for l in range(layers):
        each(chunks, lambda i: halo_each(l, i, True, lambda copy: copy.wait_send()))

    def sent(o):
        @pl.when(o != seg)
        def _():
            pool_copy(seg, o).wait_send()

    each(owners, sent)

    @pl.when(seg < owners)
    def _():
        each(S - 1, lambda k: seg_copy(k, seg).wait_send())

    each(Q - 1, lambda d: cnt_copy(d).wait())

    def arrived(d):
        source = lax.rem(cfg + Q - d - 1, Q)
        each(owners, lambda o: cfg_copy(d, source, o).wait_recv())

    each(Q - 1, arrived)
    emb_out[...] = emb_all[cfg]

    def of_graph(ref, g):
        if configs % 16 == 0:
            rows = ref[:, g * configs : (g + 1) * configs, :]
        else:
            rows = ref[...].astype(f32)[:, g * configs : (g + 1) * configs, :]
        return rows.reshape(total, rows.shape[2]).astype(bf16)

    grad = jnp.zeros((feat, feat), f32)
    loss = jnp.zeros((1, 1), f32)
    for g in range(G):
        emb = of_graph(emb_all, g)
        often = of_graph(cnt_all, g).astype(f32)
        emb_t = emb.astype(f32).T.astype(bf16)
        projected = dot(emb, bilinear[...])
        stacked = dot(jnp.concatenate(split3(projected), axis=0), emb_t)
        scores = stacked[:total] + stacked[total : 2 * total] + stacked[2 * total :]
        sign = sgn[g]
        margin = 1.0 - sign * scores
        decay = jnp.exp(-jnp.abs(margin))
        soft = jnp.maximum(margin, 0.0) + jnp.log1p(decay)
        sigmoid = jnp.where(margin >= 0.0, 1.0, decay) / (1.0 + decay)
        loss = loss + jnp.sum(often * soft, axis=(0, 1), keepdims=True)
        coef = often * (-sign) * sigmoid * (1.0 / (G * P_SIZE))
        stacked = dot(jnp.concatenate(split3(coef), axis=0), emb)
        carried = stacked[:total] + stacked[total : 2 * total] + stacked[2 * total :]
        high, middle, low = split3(carried)
        grad = grad + (dot(emb_t, high) + dot(emb_t, middle) + dot(emb_t, low))
    grad_out[...] = grad
    loss_out[...] = loss * (1.0 / (G * total * P_SIZE))

    def cfg_sent(d):
        each(owners, lambda o: cfg_copy(d, cfg, o).wait_send())

    each(Q - 1, cfg_sent)


def on_device(S, Q, node_feats, adjacency, halo_rows, node_graph, layer_weights, bilinear, partners, ranking):
    configs, nodes, feat = node_feats.shape
    rim, layers = halo_rows.shape[2], layer_weights.shape[0]
    unroll = 4
    chunks = configs // unroll
    own_rows = max(16, G * configs // S)
    owners = G * configs // own_rows
    total = Q * configs
    wide = nodes + 2 * rim
    sizes = (S, Q, configs, nodes, feat, rim, layers, unroll, own_rows, owners)
    vmem = pl.BlockSpec(memory_space=pltpu.VMEM)
    dma = pltpu.SemaphoreType.DMA
    emb, grad, loss = pl.pallas_call(
        functools.partial(kernel, sizes),
        out_shape=(
            jax.ShapeDtypeStruct((G * configs, feat), bf16),
            jax.ShapeDtypeStruct((feat, feat), f32),
            jax.ShapeDtypeStruct((1, 1), f32),
        ),
        in_specs=[pl.BlockSpec(memory_space=pl.ANY)] * 8,
        out_specs=(vmem, vmem, vmem),
        scratch_shapes=[pltpu.VMEM((configs, wide, feat), bf16)] * 3
        + [
            pltpu.VMEM((layers, configs, 2 * rim, feat), bf16),
            pltpu.VMEM((G * configs, feat), f32),
            pltpu.VMEM((S, own_rows, feat), f32),
            pltpu.VMEM((Q, G * configs, feat), bf16),
            pltpu.VMEM((Q, G * configs, total), bf16),
            pltpu.VMEM((G, total, total), f32),
            pltpu.VMEM((nodes, wide), bf16),
            pltpu.VMEM((2 * rim, nodes), bf16),
            pltpu.VMEM((16, nodes), bf16),
            pltpu.VMEM((layers, feat, feat), bf16),
            pltpu.VMEM((nodes, LANES), f32),
            pltpu.VMEM((wide, nodes), jnp.int32),
            pltpu.VMEM((2, rim), jnp.int32),
            pltpu.VMEM((1, nodes), jnp.int32),
            pltpu.VMEM((layers, feat, feat), bf16),
            pltpu.VMEM((feat, feat), bf16),
            pltpu.VMEM((G * configs, partners.shape[2]), jnp.int32),
            pltpu.VMEM((G, total), jnp.int32),
            dma((7,)),
            dma((chunks,)),
            dma((layers, 2, chunks)),
            dma((layers, 2, chunks)),
            dma((owners,)),
            dma((S,)),
            dma((S - 1,)),
            dma((owners,)),
            dma((Q - 1, owners)),
            dma((Q - 1, owners)),
            dma((Q - 1,)),
            dma((Q - 1,)),
        ],
        compiler_params=pltpu.CompilerParams(
            collective_id=0, has_side_effects=True, vmem_limit_bytes=63 * 1024 * 1024
        ),
    )(
        node_feats,
        adjacency.T,
        halo_rows.reshape(2, rim),
        node_graph.reshape(1, nodes),
        layer_weights,
        bilinear,
        partners.reshape(G * configs, partners.shape[2]),
        ranking,
    )
    return emb.reshape(G, configs, feat), grad, loss.reshape(())


def solution(mesh):
    placed = (
        P("cfg", "seg", None),
        P("seg", None),
        P("seg", None, None),
        P("seg"),
        P(),
        P(),
        P(None, "cfg", None),
        P(),
    )
    return jax.shard_map(
        functools.partial(on_device, mesh.shape["seg"], mesh.shape["cfg"]),
        mesh=mesh,
        in_specs=placed,
        out_specs=(P(None, "cfg", None), P(), P()),
        check_vma=False,
    )
```

```python
import functools

import jax
import jax.numpy as jnp
from jax import lax
from jax.experimental import pallas as pl
from jax.experimental.pallas import tpu as pltpu
from jax.sharding import PartitionSpec as P

P_SIZE = 64
G = 4
LANES = 128
eps = 1e-06
MESH = pl.DeviceIdType.MESH
f32, bf16 = jnp.float32, jnp.bfloat16


def dot(a, b):
    return jnp.dot(a, b, preferred_element_type=f32)


def split3(values):
    high = values.astype(bf16)
    rest = values - high.astype(f32)
    middle = rest.astype(bf16)
    low = (rest - middle.astype(f32)).astype(bf16)
    return high, middle, low


def each(count, fn):
    lax.fori_loop(0, count, lambda i, c: (fn(i), c)[1], 0)


def column(row, size):
    rows = lax.broadcasted_iota(jnp.int32, (size, size), 0)
    lanes = lax.broadcasted_iota(jnp.int32, (size, size), 1)
    return jnp.sum(jnp.where(rows == lanes, jnp.broadcast_to(row, (size, size)), 0.0), axis=1, keepdims=True)


def kernel(
    sizes,
    feats, *rest,
):
    compute(sizes, feats, rest[:7], *rest[7:])


def compute(
    sizes, feats, sources,
    emb_out, grad_out, loss_out,
    ext0, ext1, ext2, outbox, pooled, parts, emb_all, cnt_all, sgn, adj_mat, pick, member, half_w, eps_wide,
    adjacency, halo_rows, node_graph, weights, bilinear, partners, ranking, small_sem,
    in_sem, halo_send, halo_recv, pool_send, pool_recv, seg_send, seg_recv, cfg_send, cfg_recv, cnt_send, cnt_recv,
):
    S, Q, configs, nodes, feat, rim, layers, unroll, own_rows, owners = sizes
    exts = (ext0, ext1, ext2)
    chunks = configs // unroll
    total = Q * configs
    seg, cfg = lax.axis_index("seg"), lax.axis_index("cfg")

    barrier = pltpu.get_barrier_semaphore()

    def greet(axis, me, count):
        def one(k):
            pl.semaphore_signal(barrier, inc=1, device_id={axis: lax.rem(me + k + 1, count)}, device_id_type=MESH)
        each(count - 1, one)

    greet("seg", seg, S)
    greet("cfg", cfg, Q)

    copies = [
        pltpu.make_async_copy(source, target, small_sem.at[n])
        for n, (source, target) in enumerate(
            zip(sources, (adjacency, halo_rows, node_graph, weights, bilinear, partners, ranking))
        )
    ]
    for copy in copies:
        copy.start()

    def load(i):
        return pltpu.make_async_copy(
            feats.at[pl.ds(i * unroll, unroll)],
            ext0.at[pl.ds(i * unroll, unroll), pl.ds(rim, nodes)],
            in_sem.at[i],
        )

    each(chunks, lambda i: load(i).start())

    for copy in copies:
        copy.wait()
    wide = nodes + 2 * rim
    padded = -(-wide // LANES) * LANES
    turned = jnp.concatenate([adjacency[...].astype(f32), jnp.zeros((padded - wide, nodes), f32)], axis=0)
    adj = turned.T[:, :wide]
    degree = jnp.sum(adj, axis=1, keepdims=True)
    rows = lax.broadcasted_iota(jnp.int32, adj.shape, 0)
    lanes = lax.broadcasted_iota(jnp.int32, adj.shape, 1)
    adj_mat[...] = (adj + jnp.where(lanes == rows + rim, 1.0, 0.0)).astype(bf16)
    eps_wide[...] = jnp.broadcast_to(eps * (1.0 + degree) * (1.0 + degree), (nodes, LANES))
    half_w[...] = (weights[...].astype(f32) * 0.5).astype(bf16)
    node_ids = lax.broadcasted_iota(jnp.int32, (rim, nodes), 1).astype(f32)
    for side in range(2):
        wanted = column(halo_rows[side : side + 1, :].astype(f32), rim)
        pick[side * rim : (side + 1) * rim, :] = jnp.where(node_ids == wanted, 1.0, 0.0).astype(bf16)
    graph_ids = lax.broadcasted_iota(jnp.int32, (16, nodes), 0)
    member[...] = jnp.where(graph_ids == jnp.broadcast_to(node_graph[...], (16, nodes)), 1.0, 0.0).astype(bf16)

    @pl.when(seg == 0)
    def _():
        for ext in exts:
            ext[:, 0:rim, :] = jnp.zeros((configs, rim, feat), bf16)

    @pl.when(seg == S - 1)
    def _():
        for ext in exts:
            ext[:, rim + nodes : 2 * rim + nodes, :] = jnp.zeros((configs, rim, feat), bf16)

    pl.semaphore_wait(barrier, S + Q - 2)

    def halo_copy(l, i, side):
        batch = pl.ds(i * unroll, unroll)
        return pltpu.make_async_remote_copy(
            src_ref=outbox.at[l, batch, pl.ds(side * rim, rim)],
            dst_ref=exts[l].at[batch, pl.ds(0 if side else rim + nodes, rim)],
            send_sem=halo_send.at[l, side, i],
            recv_sem=halo_recv.at[l, side, i],
            device_id={"seg": seg + 1 if side else seg - 1},
            device_id_type=MESH,
        )

    def halo_each(l, i, sends, act):
        up, down = seg < S - 1, seg > 0

        @pl.when(down if sends else up)
        def _():
            act(halo_copy(l, i, 0))

        @pl.when(up if sends else down)
        def _():
            act(halo_copy(l, i, 1))

    def first(i):
        load(i).wait()
        ids = [i * unroll + u for u in range(unroll)]
        blocks = [ext0[c, rim : rim + nodes, :] for c in ids]
        picked = [dot(pick[...], block).astype(bf16) for block in blocks]
        for c, rows in zip(ids, picked):
            outbox[0, c] = rows
        halo_each(0, i, True, lambda copy: copy.start())

    each(chunks, first)

    def layer(l, i):
        halo_each(l, i, False, lambda copy: copy.wait_recv())
        ids = [i * unroll + u for u in range(unroll)]
        before = [exts[l][c] for c in ids]
        summed = [dot(adj_mat[...], block) for block in before]
        normed = []
        for values in summed:
            square = jnp.sum(values * values, axis=1, keepdims=True) * (1.0 / feat)
            scale = lax.rsqrt(jnp.broadcast_to(square, eps_wide.shape) + eps_wide[...])
            normed.append((values * jnp.tile(scale, (1, feat // LANES))).astype(bf16))
        halves = dot(jnp.concatenate(normed, axis=0), half_w[l])
        hidden = []
        for u in range(unroll):
            half = halves[u * nodes : (u + 1) * nodes]
            own = before[u][rim : rim + nodes].astype(f32)
            hidden.append((own + (half + half * jnp.tanh(half))).astype(bf16))
        if l < layers - 1:
            picked = [dot(pick[...], values).astype(bf16) for values in hidden]
            for c, values, rows in zip(ids, hidden, picked):
                exts[l + 1][c, rim : rim + nodes, :] = values
                outbox[l + 1, c] = rows
        else:
            sums = [dot(member[...], values) for values in hidden]
            for c, values in zip(ids, sums):
                for g in range(G):
                    pooled[pl.ds(g * configs + c, 1), :] = values[g : g + 1, :]
        if l < layers - 1:
            halo_each(l + 1, i, True, lambda copy: copy.start())

    for l in range(layers - 1):
        each(chunks, functools.partial(layer, l))

    def pool_copy(source, o):
        return pltpu.make_async_remote_copy(
            src_ref=pooled.at[pl.ds(o * own_rows, own_rows)],
            dst_ref=parts.at[source],
            send_sem=pool_send.at[o],
            recv_sem=pool_recv.at[source],
            device_id={"seg": o},
            device_id_type=MESH,
        )

    groups = max(1, configs // own_rows)
    per_group = chunks // groups

    def last_group(p):
        each(per_group, lambda j: layer(layers - 1, p * per_group + j))

        def send(k):
            o = k * groups + p

            @pl.when(o != seg)
            def _():
                pool_copy(seg, o).start()

        each(owners // groups, send)

    each(groups, last_group)

    block = 16 if (G * configs) % 16 == 0 else 8

    def count(r):
        where = pl.ds(pl.multiple_of(r * block, block), block)
        chosen = partners[where, :]
        ids = lax.broadcasted_iota(jnp.int32, (block, total), 1)
        found = jnp.zeros((block, total), f32)
        for k in range(P_SIZE):
            found = found + jnp.where(chosen[:, k : k + 1] == ids, 1.0, 0.0)
        cnt_all[cfg, where, :] = found.astype(bf16)

    each(G * configs // block, count)

    def cnt_copy(d):
        return pltpu.make_async_remote_copy(
            src_ref=cnt_all.at[cfg],
            dst_ref=cnt_all.at[cfg],
            send_sem=cnt_send.at[d],
            recv_sem=cnt_recv.at[d],
            device_id={"cfg": lax.rem(cfg + d + 1, Q)},
            device_id_type=MESH,
        )

    each(Q - 1, lambda d: cnt_copy(d).start())

    for g in range(G):
        theirs = jnp.broadcast_to(ranking[g : g + 1, :].astype(f32), (total, total))
        ahead = theirs - column(ranking[g : g + 1, :].astype(f32), total)
        sgn[g] = jnp.where(ahead > 0.0, 1.0, jnp.where(ahead < 0.0, -1.0, 0.0))

    def emb_block(q, o):
        return emb_all.at[q, pl.ds(o * own_rows, own_rows)]

    def seg_copy(k, o):
        return pltpu.make_async_remote_copy(
            src_ref=emb_block(cfg, o),
            dst_ref=emb_block(cfg, o),
            send_sem=seg_send.at[k],
            recv_sem=seg_recv.at[o],
            device_id={"seg": lax.rem(seg + k + 1, S)},
            device_id_type=MESH,
        )

    def cfg_copy(d, q, o):
        return pltpu.make_async_remote_copy(
            src_ref=emb_block(q, o),
            dst_ref=emb_block(q, o),
            send_sem=cfg_send.at[d, o],
            recv_sem=cfg_recv.at[d, o],
            device_id={"cfg": lax.rem(cfg + d + 1, Q)},
            device_id_type=MESH,
        )

    @pl.when(seg < owners)
    def _():
        parts[seg] = pooled[pl.ds(pl.multiple_of(seg * own_rows, own_rows), own_rows), :]

        def arrive(k):
            pool_copy(lax.rem(seg + k + 1, S), seg).wait_recv()

        each(S - 1, arrive)
        summed = parts[0]
        for s in range(1, S):
            summed = summed + parts[s]
        square = jnp.sum(summed * summed, axis=1, keepdims=True) * (1.0 / feat)
        mine = pl.ds(pl.multiple_of(seg * own_rows, own_rows), own_rows)
        emb_all[cfg, mine, :] = (summed * lax.rsqrt(square + eps)).astype(bf16)
        each(S - 1, lambda k: seg_copy(k, seg).start())

    def forward(k):
        o = lax.rem(seg + k, owners)

        @pl.when(o != seg)
        def _():
            seg_copy(0, o).wait_recv()

        each(Q - 1, lambda d: cfg_copy(d, cfg, o).start())

    each(owners, forward)

    for l in range(layers):
        each(chunks, lambda i: halo_each(l, i, True, lambda copy: copy.wait_send()))

    def sent(o):
        @pl.when(o != seg)
        def _():
            pool_copy(seg, o).wait_send()

    each(owners, sent)

    @pl.when(seg < owners)
    def _():
        each(S - 1, lambda k: seg_copy(k, seg).wait_send())

    each(Q - 1, lambda d: cnt_copy(d).wait())

    def arrived(d):
        source = lax.rem(cfg + Q - d - 1, Q)
        each(owners, lambda o: cfg_copy(d, source, o).wait_recv())

    each(Q - 1, arrived)
    emb_out[...] = emb_all[cfg]

    def of_graph(ref, g):
        if configs % 16 == 0:
            rows = ref[:, g * configs : (g + 1) * configs, :]
        else:
            rows = ref[...].astype(f32)[:, g * configs : (g + 1) * configs, :]
        return rows.reshape(total, rows.shape[2]).astype(bf16)

    grad = jnp.zeros((feat, feat), f32)
    loss = jnp.zeros((1, 1), f32)
    for g in range(G):
        emb = of_graph(emb_all, g)
        often = of_graph(cnt_all, g).astype(f32)
        emb_t = emb.astype(f32).T.astype(bf16)
        projected = dot(emb, bilinear[...])
        stacked = dot(jnp.concatenate(split3(projected), axis=0), emb_t)
        scores = stacked[:total] + stacked[total : 2 * total] + stacked[2 * total :]
        sign = sgn[g]
        margin = 1.0 - sign * scores
        decay = jnp.exp(-jnp.abs(margin))
        soft = jnp.maximum(margin, 0.0) + jnp.log1p(decay)
        sigmoid = jnp.where(margin >= 0.0, 1.0, decay) / (1.0 + decay)
        loss = loss + jnp.sum(often * soft, axis=(0, 1), keepdims=True)
        coef = often * (-sign) * sigmoid * (1.0 / (G * P_SIZE))
        stacked = dot(jnp.concatenate(split3(coef), axis=0), emb)
        carried = stacked[:total] + stacked[total : 2 * total] + stacked[2 * total :]
        high, middle, low = split3(carried)
        grad = grad + (dot(emb_t, high) + dot(emb_t, middle) + dot(emb_t, low))
    grad_out[...] = grad
    loss_out[...] = loss * (1.0 / (G * total * P_SIZE))

    def cfg_sent(d):
        each(owners, lambda o: cfg_copy(d, cfg, o).wait_send())

    each(Q - 1, cfg_sent)


def on_device(S, Q, node_feats, adjacency, halo_rows, node_graph, layer_weights, bilinear, partners, ranking):
    configs, nodes, feat = node_feats.shape
    rim, layers = halo_rows.shape[2], layer_weights.shape[0]
    unroll = 8 if configs % 8 == 0 else 4
    chunks = configs // unroll
    own_rows = max(16, G * configs // S)
    owners = G * configs // own_rows
    total = Q * configs
    wide = nodes + 2 * rim
    sizes = (S, Q, configs, nodes, feat, rim, layers, unroll, own_rows, owners)
    vmem = pl.BlockSpec(memory_space=pltpu.VMEM)
    dma = pltpu.SemaphoreType.DMA
    emb, grad, loss = pl.pallas_call(
        functools.partial(kernel, sizes),
        out_shape=(
            jax.ShapeDtypeStruct((G * configs, feat), bf16),
            jax.ShapeDtypeStruct((feat, feat), f32),
            jax.ShapeDtypeStruct((1, 1), f32),
        ),
        in_specs=[pl.BlockSpec(memory_space=pl.ANY)] * 8,
        out_specs=(vmem, vmem, vmem),
        scratch_shapes=[pltpu.VMEM((configs, wide, feat), bf16)] * 3
        + [
            pltpu.VMEM((layers, configs, 2 * rim, feat), bf16),
            pltpu.VMEM((G * configs, feat), f32),
            pltpu.VMEM((S, own_rows, feat), f32),
            pltpu.VMEM((Q, G * configs, feat), bf16),
            pltpu.VMEM((Q, G * configs, total), bf16),
            pltpu.VMEM((G, total, total), f32),
            pltpu.VMEM((nodes, wide), bf16),
            pltpu.VMEM((2 * rim, nodes), bf16),
            pltpu.VMEM((16, nodes), bf16),
            pltpu.VMEM((layers, feat, feat), bf16),
            pltpu.VMEM((nodes, LANES), f32),
            pltpu.VMEM((wide, nodes), jnp.int32),
            pltpu.VMEM((2, rim), jnp.int32),
            pltpu.VMEM((1, nodes), jnp.int32),
            pltpu.VMEM((layers, feat, feat), bf16),
            pltpu.VMEM((feat, feat), bf16),
            pltpu.VMEM((G * configs, partners.shape[2]), jnp.int32),
            pltpu.VMEM((G, total), jnp.int32),
            dma((7,)),
            dma((chunks,)),
            dma((layers, 2, chunks)),
            dma((layers, 2, chunks)),
            dma((owners,)),
            dma((S,)),
            dma((S - 1,)),
            dma((owners,)),
            dma((Q - 1, owners)),
            dma((Q - 1, owners)),
            dma((Q - 1,)),
            dma((Q - 1,)),
        ],
        compiler_params=pltpu.CompilerParams(
            collective_id=0, has_side_effects=True, vmem_limit_bytes=63 * 1024 * 1024
        ),
    )(
        node_feats,
        adjacency.T,
        halo_rows.reshape(2, rim),
        node_graph.reshape(1, nodes),
        layer_weights,
        bilinear,
        partners.reshape(G * configs, partners.shape[2]),
        ranking,
    )
    return emb.reshape(G, configs, feat), grad, loss.reshape(())


def solution(mesh):
    placed = (
        P("cfg", "seg", None),
        P("seg", None),
        P("seg", None, None),
        P("seg"),
        P(),
        P(),
        P(None, "cfg", None),
        P(),
    )
    return jax.shard_map(
        functools.partial(on_device, mesh.shape["seg"], mesh.shape["cfg"]),
        mesh=mesh,
        in_specs=placed,
        out_specs=(P(None, "cfg", None), P(), P()),
        check_vma=False,
    )
```

```python
import functools

import jax
import jax.numpy as jnp
from jax import lax
from jax.experimental import pallas as pl
from jax.experimental.pallas import tpu as pltpu
from jax.sharding import PartitionSpec as P

P_SIZE = 64
G = 4
LANES = 128
eps = 1e-06
MESH = pl.DeviceIdType.MESH
f32, bf16 = jnp.float32, jnp.bfloat16


def dot(a, b):
    return jnp.dot(a, b, preferred_element_type=f32)


def split3(values):
    high = values.astype(bf16)
    rest = values - high.astype(f32)
    middle = rest.astype(bf16)
    low = (rest - middle.astype(f32)).astype(bf16)
    return high, middle, low


def each(count, fn):
    lax.fori_loop(0, count, lambda i, c: (fn(i), c)[1], 0)


def column(row, size):
    rows = lax.broadcasted_iota(jnp.int32, (size, size), 0)
    lanes = lax.broadcasted_iota(jnp.int32, (size, size), 1)
    return jnp.sum(jnp.where(rows == lanes, jnp.broadcast_to(row, (size, size)), 0.0), axis=1, keepdims=True)


def kernel(
    sizes,
    feats, *rest,
):
    compute(sizes, feats, rest[:7], *rest[7:])


def compute(
    sizes, feats, sources,
    emb_out, grad_out, loss_out,
    ext0, ext1, ext2, outbox, pooled, parts, emb_all, cnt_all, sgn, adj_mat, pick, member, half_w, eps_wide,
    adjacency, halo_rows, node_graph, weights, bilinear, partners, ranking, small_sem,
    in_sem, halo_send, halo_recv, pool_send, pool_recv, seg_send, seg_recv, cfg_send, cfg_recv, cnt_send, cnt_recv,
):
    S, Q, configs, nodes, feat, rim, layers, unroll, own_rows, owners = sizes
    exts = (ext0, ext1, ext2)
    chunks = configs // unroll
    total = Q * configs
    seg, cfg = lax.axis_index("seg"), lax.axis_index("cfg")

    barrier = pltpu.get_barrier_semaphore()

    def greet(axis, me, count):
        def one(k):
            pl.semaphore_signal(barrier, inc=1, device_id={axis: lax.rem(me + k + 1, count)}, device_id_type=MESH)
        each(count - 1, one)

    greet("seg", seg, S)
    greet("cfg", cfg, Q)

    copies = [
        pltpu.make_async_copy(source, target, small_sem.at[n])
        for n, (source, target) in enumerate(
            zip(sources, (adjacency, halo_rows, node_graph, weights, bilinear, partners, ranking))
        )
    ]
    for copy in copies:
        copy.start()

    def load(i):
        return pltpu.make_async_copy(
            feats.at[pl.ds(i * unroll, unroll)],
            ext0.at[pl.ds(i * unroll, unroll), pl.ds(rim, nodes)],
            in_sem.at[i],
        )

    each(chunks, lambda i: load(i).start())

    for copy in copies:
        copy.wait()
    wide = nodes + 2 * rim
    padded = -(-wide // LANES) * LANES
    turned = jnp.concatenate([adjacency[...].astype(f32), jnp.zeros((padded - wide, nodes), f32)], axis=0)
    adj = turned.T[:, :wide]
    degree = jnp.sum(adj, axis=1, keepdims=True)
    rows = lax.broadcasted_iota(jnp.int32, adj.shape, 0)
    lanes = lax.broadcasted_iota(jnp.int32, adj.shape, 1)
    adj_mat[...] = (adj + jnp.where(lanes == rows + rim, 1.0, 0.0)).astype(bf16)
    eps_wide[...] = jnp.broadcast_to(eps * (1.0 + degree) * (1.0 + degree), (nodes, LANES))
    half_w[...] = (weights[...].astype(f32) * 0.5).astype(bf16)
    node_ids = lax.broadcasted_iota(jnp.int32, (rim, nodes), 1).astype(f32)
    for side in range(2):
        wanted = column(halo_rows[side : side + 1, :].astype(f32), rim)
        pick[side * rim : (side + 1) * rim, :] = jnp.where(node_ids == wanted, 1.0, 0.0).astype(bf16)
    graph_ids = lax.broadcasted_iota(jnp.int32, (16, nodes), 0)
    member[...] = jnp.where(graph_ids == jnp.broadcast_to(node_graph[...], (16, nodes)), 1.0, 0.0).astype(bf16)

    @pl.when(seg == 0)
    def _():
        for ext in exts:
            ext[:, 0:rim, :] = jnp.zeros((configs, rim, feat), bf16)

    @pl.when(seg == S - 1)
    def _():
        for ext in exts:
            ext[:, rim + nodes : 2 * rim + nodes, :] = jnp.zeros((configs, rim, feat), bf16)

    pl.semaphore_wait(barrier, S + Q - 2)

    def halo_copy(l, i, side):
        batch = pl.ds(i * unroll, unroll)
        return pltpu.make_async_remote_copy(
            src_ref=outbox.at[l, batch, pl.ds(side * rim, rim)],
            dst_ref=exts[l].at[batch, pl.ds(0 if side else rim + nodes, rim)],
            send_sem=halo_send.at[l, side, i],
            recv_sem=halo_recv.at[l, side, i],
            device_id={"seg": seg + 1 if side else seg - 1},
            device_id_type=MESH,
        )

    def halo_each(l, i, sends, act):
        up, down = seg < S - 1, seg > 0

        @pl.when(down if sends else up)
        def _():
            act(halo_copy(l, i, 0))

        @pl.when(up if sends else down)
        def _():
            act(halo_copy(l, i, 1))

    def first(i):
        load(i).wait()
        ids = [i * unroll + u for u in range(unroll)]
        blocks = [ext0[c, rim : rim + nodes, :] for c in ids]
        picked = [dot(pick[...], block).astype(bf16) for block in blocks]
        for c, rows in zip(ids, picked):
            outbox[0, c] = rows
        halo_each(0, i, True, lambda copy: copy.start())

    each(chunks, first)

    def layer(l, i):
        halo_each(l, i, False, lambda copy: copy.wait_recv())
        ids = [i * unroll + u for u in range(unroll)]
        before = [exts[l][c] for c in ids]
        summed = [dot(adj_mat[...], block) for block in before]
        normed = []
        for values in summed:
            square = jnp.sum(values * values, axis=1, keepdims=True) * (1.0 / feat)
            scale = lax.rsqrt(jnp.broadcast_to(square, eps_wide.shape) + eps_wide[...])
            normed.append((values * jnp.tile(scale, (1, feat // LANES))).astype(bf16))
        halves = dot(jnp.concatenate(normed, axis=0), half_w[l])
        hidden = []
        for u in range(unroll):
            half = halves[u * nodes : (u + 1) * nodes]
            own = before[u][rim : rim + nodes].astype(f32)
            hidden.append((own + (half + half * jnp.tanh(half))).astype(bf16))
        if l < layers - 1:
            picked = [dot(pick[...], values).astype(bf16) for values in hidden]
            for c, values, rows in zip(ids, hidden, picked):
                exts[l + 1][c, rim : rim + nodes, :] = values
                outbox[l + 1, c] = rows
        else:
            sums = [dot(member[...], values) for values in hidden]
            for c, values in zip(ids, sums):
                for g in range(G):
                    pooled[pl.ds(g * configs + c, 1), :] = values[g : g + 1, :]
        if l < layers - 1:
            halo_each(l + 1, i, True, lambda copy: copy.start())

    for l in range(layers - 1):
        each(chunks, functools.partial(layer, l))

    def pool_copy(source, o):
        return pltpu.make_async_remote_copy(
            src_ref=pooled.at[pl.ds(o * own_rows, own_rows)],
            dst_ref=parts.at[source],
            send_sem=pool_send.at[o],
            recv_sem=pool_recv.at[source],
            device_id={"seg": o},
            device_id_type=MESH,
        )

    groups = max(1, configs // own_rows)
    per_group = chunks // groups

    def last_group(p):
        each(per_group, lambda j: layer(layers - 1, p * per_group + j))

        def send(k):
            o = k * groups + p

            @pl.when(o != seg)
            def _():
                pool_copy(seg, o).start()

        each(owners // groups, send)

    each(groups, last_group)

    block = 16 if (G * configs) % 16 == 0 else 8

    def count(r):
        where = pl.ds(pl.multiple_of(r * block, block), block)
        chosen = partners[where, :]
        ids = lax.broadcasted_iota(jnp.int32, (block, total), 1)
        found = jnp.zeros((block, total), f32)
        for k in range(P_SIZE):
            found = found + jnp.where(chosen[:, k : k + 1] == ids, 1.0, 0.0)
        cnt_all[cfg, where, :] = found.astype(bf16)

    each(G * configs // block, count)

    def cnt_copy(d):
        return pltpu.make_async_remote_copy(
            src_ref=cnt_all.at[cfg],
            dst_ref=cnt_all.at[cfg],
            send_sem=cnt_send.at[d],
            recv_sem=cnt_recv.at[d],
            device_id={"cfg": lax.rem(cfg + d + 1, Q)},
            device_id_type=MESH,
        )

    each(Q - 1, lambda d: cnt_copy(d).start())

    for g in range(G):
        theirs = jnp.broadcast_to(ranking[g : g + 1, :].astype(f32), (total, total))
        ahead = theirs - column(ranking[g : g + 1, :].astype(f32), total)
        sgn[g] = jnp.where(ahead > 0.0, 1.0, jnp.where(ahead < 0.0, -1.0, 0.0))

    for l in range(layers):
        each(chunks, lambda i: halo_each(l, i, True, lambda copy: copy.wait_send()))

    def emb_block(q, o):
        return emb_all.at[q, pl.ds(o * own_rows, own_rows)]

    def seg_copy(k, o):
        return pltpu.make_async_remote_copy(
            src_ref=emb_block(cfg, o),
            dst_ref=emb_block(cfg, o),
            send_sem=seg_send.at[k],
            recv_sem=seg_recv.at[o],
            device_id={"seg": lax.rem(seg + k + 1, S)},
            device_id_type=MESH,
        )

    def cfg_copy(d, q, o):
        return pltpu.make_async_remote_copy(
            src_ref=emb_block(q, o),
            dst_ref=emb_block(q, o),
            send_sem=cfg_send.at[d, o],
            recv_sem=cfg_recv.at[d, o],
            device_id={"cfg": lax.rem(cfg + d + 1, Q)},
            device_id_type=MESH,
        )

    @pl.when(seg < owners)
    def _():
        parts[seg] = pooled[pl.ds(pl.multiple_of(seg * own_rows, own_rows), own_rows), :]

        def arrive(k):
            pool_copy(lax.rem(seg + k + 1, S), seg).wait_recv()

        each(S - 1, arrive)
        summed = parts[0]
        for s in range(1, S):
            summed = summed + parts[s]
        square = jnp.sum(summed * summed, axis=1, keepdims=True) * (1.0 / feat)
        mine = pl.ds(pl.multiple_of(seg * own_rows, own_rows), own_rows)
        emb_all[cfg, mine, :] = (summed * lax.rsqrt(square + eps)).astype(bf16)
        each(S - 1, lambda k: seg_copy(k, seg).start())

    def forward(o):
        @pl.when(o != seg)
        def _():
            seg_copy(0, o).wait_recv()

        each(Q - 1, lambda d: cfg_copy(d, cfg, o).start())

    each(owners, forward)

    emb_out[...] = emb_all[cfg]

    def sent(o):
        @pl.when(o != seg)
        def _():
            pool_copy(seg, o).wait_send()

    each(Q - 1, lambda d: cnt_copy(d).wait())

    def arrived(first, last):
        def one(d):
            source = lax.rem(cfg + Q - d - 1, Q)
            each(last - first, lambda k: cfg_copy(d, source, first + k).wait_recv())

        each(Q - 1, one)

    def of_graph(ref, g):
        if configs % 16 == 0:
            rows = ref[:, g * configs : (g + 1) * configs, :]
        else:
            rows = ref[...].astype(f32)[:, g * configs : (g + 1) * configs, :]
        return rows.reshape(total, rows.shape[2]).astype(bf16)

    grad = jnp.zeros((feat, feat), f32)
    loss = jnp.zeros((1, 1), f32)
    paired = (2 * configs) % own_rows == 0
    if not paired:
        arrived(0, owners)
    for g in range(G):
        if paired and g % 2 == 0:
            arrived(g * configs // own_rows, (g + 2) * configs // own_rows)
        emb = of_graph(emb_all, g)
        often = of_graph(cnt_all, g).astype(f32)
        emb_t = emb.astype(f32).T.astype(bf16)
        projected = dot(emb, bilinear[...])
        stacked = dot(jnp.concatenate(split3(projected), axis=0), emb_t)
        scores = stacked[:total] + stacked[total : 2 * total] + stacked[2 * total :]
        sign = sgn[g]
        margin = 1.0 - sign * scores
        decay = jnp.exp(-jnp.abs(margin))
        soft = jnp.maximum(margin, 0.0) + jnp.log1p(decay)
        sigmoid = jnp.where(margin >= 0.0, 1.0, decay) / (1.0 + decay)
        loss = loss + jnp.sum(often * soft, axis=(0, 1), keepdims=True)
        coef = often * (-sign) * sigmoid * (1.0 / (G * P_SIZE))
        stacked = dot(jnp.concatenate(split3(coef), axis=0), emb)
        carried = stacked[:total] + stacked[total : 2 * total] + stacked[2 * total :]
        high, middle, low = split3(carried)
        grad = grad + (dot(emb_t, high) + dot(emb_t, middle) + dot(emb_t, low))
    grad_out[...] = grad
    loss_out[...] = loss * (1.0 / (G * total * P_SIZE))

    def cfg_sent(d):
        each(owners, lambda o: cfg_copy(d, cfg, o).wait_send())

    each(Q - 1, cfg_sent)
    each(owners, sent)

    @pl.when(seg < owners)
    def _():
        each(S - 1, lambda k: seg_copy(k, seg).wait_send())


def hand_over(emb, grad, emb_out, grad_out, sems):
    moves = [
        pltpu.make_async_copy(emb, emb_out, sems.at[0]),
        pltpu.make_async_copy(grad, grad_out, sems.at[1]),
    ]
    for move in moves:
        move.start()
    for move in moves:
        move.wait()


def on_device(S, Q, node_feats, adjacency, halo_rows, node_graph, layer_weights, bilinear, partners, ranking):
    configs, nodes, feat = node_feats.shape
    rim, layers = halo_rows.shape[2], layer_weights.shape[0]
    unroll = 8 if configs % 8 == 0 else 4
    chunks = configs // unroll
    own_rows = max(16, G * configs // S)
    owners = G * configs // own_rows
    total = Q * configs
    wide = nodes + 2 * rim
    sizes = (S, Q, configs, nodes, feat, rim, layers, unroll, own_rows, owners)
    vmem = pl.BlockSpec(memory_space=pltpu.VMEM)
    dma = pltpu.SemaphoreType.DMA
    emb, grad, loss = pl.pallas_call(
        functools.partial(kernel, sizes),
        out_shape=(
            jax.ShapeDtypeStruct((G * configs, feat), bf16),
            jax.ShapeDtypeStruct((feat, feat), f32),
            jax.ShapeDtypeStruct((1, 1), f32),
        ),
        in_specs=[pl.BlockSpec(memory_space=pl.ANY)] * 8,
        out_specs=(vmem, vmem, vmem),
        scratch_shapes=[pltpu.VMEM((configs, wide, feat), bf16)] * 3
        + [
            pltpu.VMEM((layers, configs, 2 * rim, feat), bf16),
            pltpu.VMEM((G * configs, feat), f32),
            pltpu.VMEM((S, own_rows, feat), f32),
            pltpu.VMEM((Q, G * configs, feat), bf16),
            pltpu.VMEM((Q, G * configs, total), bf16),
            pltpu.VMEM((G, total, total), f32),
            pltpu.VMEM((nodes, wide), bf16),
            pltpu.VMEM((2 * rim, nodes), bf16),
            pltpu.VMEM((16, nodes), bf16),
            pltpu.VMEM((layers, feat, feat), bf16),
            pltpu.VMEM((nodes, LANES), f32),
            pltpu.VMEM((wide, nodes), jnp.int32),
            pltpu.VMEM((2, rim), jnp.int32),
            pltpu.VMEM((1, nodes), jnp.int32),
            pltpu.VMEM((layers, feat, feat), bf16),
            pltpu.VMEM((feat, feat), bf16),
            pltpu.VMEM((G * configs, partners.shape[2]), jnp.int32),
            pltpu.VMEM((G, total), jnp.int32),
            dma((7,)),
            dma((chunks,)),
            dma((layers, 2, chunks)),
            dma((layers, 2, chunks)),
            dma((owners,)),
            dma((S,)),
            dma((S - 1,)),
            dma((owners,)),
            dma((Q - 1, owners)),
            dma((Q - 1, owners)),
            dma((Q - 1,)),
            dma((Q - 1,)),
        ],
        compiler_params=pltpu.CompilerParams(
            collective_id=0, has_side_effects=True, vmem_limit_bytes=63 * 1024 * 1024
        ),
    )(
        node_feats,
        adjacency.T,
        halo_rows.reshape(2, rim),
        node_graph.reshape(1, nodes),
        layer_weights,
        bilinear,
        partners.reshape(G * configs, partners.shape[2]),
        ranking,
    )
    any_space = pl.BlockSpec(memory_space=pl.ANY)
    emb, grad = pl.pallas_call(
        hand_over,
        out_shape=(jax.ShapeDtypeStruct(emb.shape, bf16), jax.ShapeDtypeStruct(grad.shape, f32)),
        in_specs=[any_space] * 2,
        out_specs=(any_space, any_space),
        scratch_shapes=[dma((2,))],
        compiler_params=pltpu.CompilerParams(vmem_limit_bytes=63 * 1024 * 1024),
    )(emb, grad)
    return emb.reshape(G, configs, feat), grad, loss.reshape(())


def solution(mesh):
    placed = (
        P("cfg", "seg", None),
        P("seg", None),
        P("seg", None, None),
        P("seg"),
        P(),
        P(),
        P(None, "cfg", None),
        P(),
    )
    return jax.shard_map(
        functools.partial(on_device, mesh.shape["seg"], mesh.shape["cfg"]),
        mesh=mesh,
        in_specs=placed,
        out_specs=(P(None, "cfg", None), P(), P()),
        check_vma=False,
    )
```

```python
import functools

import jax
import jax.numpy as jnp
from jax import lax
from jax.experimental import pallas as pl
from jax.experimental.pallas import tpu as pltpu
from jax.sharding import PartitionSpec as P

P_SIZE = 64
G = 4
LANES = 128
eps = 1e-06
MESH = pl.DeviceIdType.MESH
f32, bf16 = jnp.float32, jnp.bfloat16


def dot(a, b):
    return jnp.dot(a, b, preferred_element_type=f32)


def split3(values):
    high = values.astype(bf16)
    rest = values - high.astype(f32)
    middle = rest.astype(bf16)
    low = (rest - middle.astype(f32)).astype(bf16)
    return high, middle, low


def each(count, fn):
    lax.fori_loop(0, count, lambda i, c: (fn(i), c)[1], 0)


def column(row, size):
    rows = lax.broadcasted_iota(jnp.int32, (size, size), 0)
    lanes = lax.broadcasted_iota(jnp.int32, (size, size), 1)
    return jnp.sum(jnp.where(rows == lanes, jnp.broadcast_to(row, (size, size)), 0.0), axis=1, keepdims=True)


def kernel(
    sizes,
    feats, *rest,
):
    compute(sizes, feats, rest[:7], *rest[7:])


def compute(
    sizes, feats, sources,
    emb_out, grad_out, loss_out,
    ext0, ext1, ext2, outbox, pooled, parts, emb_all, cnt_all, sgn, adj_mat, pick, member, half_w, eps_wide,
    adjacency, halo_rows, node_graph, weights, bilinear, partners, ranking, small_sem,
    in_sem, halo_send, halo_recv, pool_send, pool_recv, seg_send, seg_recv, cfg_send, cfg_recv, cnt_send, cnt_recv,
):
    S, Q, configs, nodes, feat, rim, layers, unroll, own_rows, owners = sizes
    exts = (ext0, ext1, ext2)
    chunks = configs // unroll
    total = Q * configs
    seg, cfg = lax.axis_index("seg"), lax.axis_index("cfg")

    barrier = pltpu.get_barrier_semaphore()

    def greet(axis, me, count):
        def one(k):
            pl.semaphore_signal(barrier, inc=1, device_id={axis: lax.rem(me + k + 1, count)}, device_id_type=MESH)
        each(count - 1, one)

    greet("seg", seg, S)
    greet("cfg", cfg, Q)

    copies = [
        pltpu.make_async_copy(source, target, small_sem.at[n])
        for n, (source, target) in enumerate(
            zip(sources, (adjacency, halo_rows, node_graph, weights, bilinear, partners, ranking))
        )
    ]
    for copy in copies:
        copy.start()

    def load(i):
        return pltpu.make_async_copy(
            feats.at[pl.ds(i * unroll, unroll)],
            ext0.at[pl.ds(i * unroll, unroll), pl.ds(rim, nodes)],
            in_sem.at[i],
        )

    each(chunks, lambda i: load(i).start())

    for copy in copies:
        copy.wait()
    wide = nodes + 2 * rim
    padded = -(-wide // LANES) * LANES
    turned = jnp.concatenate([adjacency[...].astype(f32), jnp.zeros((padded - wide, nodes), f32)], axis=0)
    adj = turned.T[:, :wide]
    degree = jnp.sum(adj, axis=1, keepdims=True)
    rows = lax.broadcasted_iota(jnp.int32, adj.shape, 0)
    lanes = lax.broadcasted_iota(jnp.int32, adj.shape, 1)
    adj_mat[...] = (adj + jnp.where(lanes == rows + rim, 1.0, 0.0)).astype(bf16)
    eps_wide[...] = jnp.broadcast_to(eps * (1.0 + degree) * (1.0 + degree), (nodes, LANES))
    half_w[...] = (weights[...].astype(f32) * 0.5).astype(bf16)
    node_ids = lax.broadcasted_iota(jnp.int32, (rim, nodes), 1).astype(f32)
    for side in range(2):
        wanted = column(halo_rows[side : side + 1, :].astype(f32), rim)
        pick[side * rim : (side + 1) * rim, :] = jnp.where(node_ids == wanted, 1.0, 0.0).astype(bf16)
    graph_ids = lax.broadcasted_iota(jnp.int32, (16, nodes), 0)
    member[...] = jnp.where(graph_ids == jnp.broadcast_to(node_graph[...], (16, nodes)), 1.0, 0.0).astype(bf16)

    @pl.when(seg == 0)
    def _():
        for ext in exts:
            ext[:, 0:rim, :] = jnp.zeros((configs, rim, feat), bf16)

    @pl.when(seg == S - 1)
    def _():
        for ext in exts:
            ext[:, rim + nodes : 2 * rim + nodes, :] = jnp.zeros((configs, rim, feat), bf16)

    pl.semaphore_wait(barrier, S + Q - 2)

    def halo_copy(l, i, side):
        batch = pl.ds(i * unroll, unroll)
        return pltpu.make_async_remote_copy(
            src_ref=outbox.at[l, batch, pl.ds(side * rim, rim)],
            dst_ref=exts[l].at[batch, pl.ds(0 if side else rim + nodes, rim)],
            send_sem=halo_send.at[l, side, i],
            recv_sem=halo_recv.at[l, side, i],
            device_id={"seg": seg + 1 if side else seg - 1},
            device_id_type=MESH,
        )

    def halo_each(l, i, sends, act):
        up, down = seg < S - 1, seg > 0

        @pl.when(down if sends else up)
        def _():
            act(halo_copy(l, i, 0))

        @pl.when(up if sends else down)
        def _():
            act(halo_copy(l, i, 1))

    def first(i):
        load(i).wait()
        ids = [i * unroll + u for u in range(unroll)]
        blocks = [ext0[c, rim : rim + nodes, :] for c in ids]
        picked = [dot(pick[...], block).astype(bf16) for block in blocks]
        for c, rows in zip(ids, picked):
            outbox[0, c] = rows
        halo_each(0, i, True, lambda copy: copy.start())

    each(chunks, first)

    def layer(l, i):
        halo_each(l, i, False, lambda copy: copy.wait_recv())
        ids = [i * unroll + u for u in range(unroll)]
        before = [exts[l][c] for c in ids]
        summed = [dot(adj_mat[...], block) for block in before]
        normed = []
        for values in summed:
            square = jnp.sum(values * values, axis=1, keepdims=True) * (1.0 / feat)
            scale = lax.rsqrt(jnp.broadcast_to(square, eps_wide.shape) + eps_wide[...])
            normed.append((values * jnp.tile(scale, (1, feat // LANES))).astype(bf16))
        halves = dot(jnp.concatenate(normed, axis=0), half_w[l])
        hidden = []
        for u in range(unroll):
            half = halves[u * nodes : (u + 1) * nodes]
            own = before[u][rim : rim + nodes].astype(f32)
            hidden.append((own + (half + half * jnp.tanh(half))).astype(bf16))
        if l < layers - 1:
            picked = [dot(pick[...], values).astype(bf16) for values in hidden]
            for c, values, rows in zip(ids, hidden, picked):
                exts[l + 1][c, rim : rim + nodes, :] = values
                outbox[l + 1, c] = rows
        else:
            sums = [dot(member[...], values) for values in hidden]
            for c, values in zip(ids, sums):
                for g in range(G):
                    pooled[pl.ds(g * configs + c, 1), :] = values[g : g + 1, :]
        if l < layers - 1:
            halo_each(l + 1, i, True, lambda copy: copy.start())

    for l in range(layers - 1):
        each(chunks, functools.partial(layer, l))

    def pool_copy(source, o):
        return pltpu.make_async_remote_copy(
            src_ref=pooled.at[pl.ds(o * own_rows, own_rows)],
            dst_ref=parts.at[source],
            send_sem=pool_send.at[o],
            recv_sem=pool_recv.at[source],
            device_id={"seg": o},
            device_id_type=MESH,
        )

    groups = max(1, configs // own_rows)
    per_group = chunks // groups

    def last_group(p):
        each(per_group, lambda j: layer(layers - 1, p * per_group + j))

        def send(k):
            o = k * groups + p

            @pl.when(o != seg)
            def _():
                pool_copy(seg, o).start()

        each(owners // groups, send)

    each(groups, last_group)

    block = 16 if (G * configs) % 16 == 0 else 8

    def count(r):
        where = pl.ds(pl.multiple_of(r * block, block), block)
        chosen = partners[where, :]
        ids = lax.broadcasted_iota(jnp.int32, (block, total), 1)
        found = jnp.zeros((block, total), f32)
        for k in range(P_SIZE):
            found = found + jnp.where(chosen[:, k : k + 1] == ids, 1.0, 0.0)
        cnt_all[cfg, where, :] = found.astype(bf16)

    each(G * configs // block, count)

    def cnt_copy(d):
        return pltpu.make_async_remote_copy(
            src_ref=cnt_all.at[cfg],
            dst_ref=cnt_all.at[cfg],
            send_sem=cnt_send.at[d],
            recv_sem=cnt_recv.at[d],
            device_id={"cfg": lax.rem(cfg + d + 1, Q)},
            device_id_type=MESH,
        )

    each(Q - 1, lambda d: cnt_copy(d).start())

    for g in range(G):
        theirs = jnp.broadcast_to(ranking[g : g + 1, :].astype(f32), (total, total))
        ahead = theirs - column(ranking[g : g + 1, :].astype(f32), total)
        sgn[g] = jnp.where(ahead > 0.0, 1.0, jnp.where(ahead < 0.0, -1.0, 0.0))

    for l in range(layers):
        each(chunks, lambda i: halo_each(l, i, True, lambda copy: copy.wait_send()))

    def emb_block(q, o):
        return emb_all.at[q, pl.ds(o * own_rows, own_rows)]

    def seg_copy(k, o):
        return pltpu.make_async_remote_copy(
            src_ref=emb_block(cfg, o),
            dst_ref=emb_block(cfg, o),
            send_sem=seg_send.at[k],
            recv_sem=seg_recv.at[o],
            device_id={"seg": lax.rem(seg + k + 1, S)},
            device_id_type=MESH,
        )

    def cfg_copy(d, q, o):
        return pltpu.make_async_remote_copy(
            src_ref=emb_block(q, o),
            dst_ref=emb_block(q, o),
            send_sem=cfg_send.at[d, o],
            recv_sem=cfg_recv.at[d, o],
            device_id={"cfg": lax.rem(cfg + d + 1, Q)},
            device_id_type=MESH,
        )

    @pl.when(seg < owners)
    def _():
        parts[seg] = pooled[pl.ds(pl.multiple_of(seg * own_rows, own_rows), own_rows), :]

        def arrive(k):
            pool_copy(lax.rem(seg + k + 1, S), seg).wait_recv()

        each(S - 1, arrive)
        summed = parts[0]
        for s in range(1, S):
            summed = summed + parts[s]
        square = jnp.sum(summed * summed, axis=1, keepdims=True) * (1.0 / feat)
        mine = pl.ds(pl.multiple_of(seg * own_rows, own_rows), own_rows)
        emb_all[cfg, mine, :] = (summed * lax.rsqrt(square + eps)).astype(bf16)
        each(S - 1, lambda k: seg_copy(k, seg).start())

    def forward(o):
        @pl.when(o != seg)
        def _():
            seg_copy(0, o).wait_recv()

        each(Q - 1, lambda d: cfg_copy(d, cfg, o).start())

    each(owners, forward)

    emb_out[...] = emb_all[cfg]

    def sent(o):
        @pl.when(o != seg)
        def _():
            pool_copy(seg, o).wait_send()

    each(Q - 1, lambda d: cnt_copy(d).wait())

    def arrived(first, last):
        def one(d):
            source = lax.rem(cfg + Q - d - 1, Q)
            each(last - first, lambda k: cfg_copy(d, source, first + k).wait_recv())

        each(Q - 1, one)

    def of_graph(ref, g):
        if configs % 16 == 0:
            rows = ref[:, g * configs : (g + 1) * configs, :]
        else:
            rows = ref[...].astype(f32)[:, g * configs : (g + 1) * configs, :]
        return rows.reshape(total, rows.shape[2]).astype(bf16)

    grad = jnp.zeros((feat, feat), f32)
    loss = jnp.zeros((1, 1), f32)
    paired = (2 * configs) % own_rows == 0
    if not paired:
        arrived(0, owners)
    for g in range(G):
        if paired and g % 2 == 0:
            arrived(g * configs // own_rows, (g + 2) * configs // own_rows)
        emb = of_graph(emb_all, g)
        often = of_graph(cnt_all, g).astype(f32)
        emb_t = emb.astype(f32).T.astype(bf16)
        projected = dot(emb, bilinear[...])
        stacked = dot(jnp.concatenate(split3(projected), axis=0), emb_t)
        scores = stacked[:total] + stacked[total : 2 * total] + stacked[2 * total :]
        sign = sgn[g]
        margin = 1.0 - sign * scores
        decay = jnp.exp(-jnp.abs(margin))
        soft = jnp.maximum(margin, 0.0) + jnp.log1p(decay)
        sigmoid = jnp.where(margin >= 0.0, 1.0, decay) / (1.0 + decay)
        loss = loss + jnp.sum(often * soft, axis=(0, 1), keepdims=True)
        coef = often * (-sign) * sigmoid * (1.0 / (G * P_SIZE))
        stacked = dot(jnp.concatenate(split3(coef), axis=0), emb)
        carried = stacked[:total] + stacked[total : 2 * total] + stacked[2 * total :]
        high, middle, low = split3(carried)
        grad = grad + (dot(emb_t, high) + dot(emb_t, middle) + dot(emb_t, low))
    grad_out[...] = grad
    loss_out[...] = loss * (1.0 / (G * total * P_SIZE))

    def cfg_sent(d):
        each(owners, lambda o: cfg_copy(d, cfg, o).wait_send())

    each(Q - 1, cfg_sent)
    each(owners, sent)

    @pl.when(seg < owners)
    def _():
        each(S - 1, lambda k: seg_copy(k, seg).wait_send())


def hand_over(emb, grad, emb_out, grad_out):
    emb_out[...] = emb[...]
    grad_out[...] = grad[...]


def on_device(S, Q, node_feats, adjacency, halo_rows, node_graph, layer_weights, bilinear, partners, ranking):
    configs, nodes, feat = node_feats.shape
    rim, layers = halo_rows.shape[2], layer_weights.shape[0]
    unroll = 8 if configs % 8 == 0 else 4
    chunks = configs // unroll
    own_rows = max(16, G * configs // S)
    owners = G * configs // own_rows
    total = Q * configs
    wide = nodes + 2 * rim
    sizes = (S, Q, configs, nodes, feat, rim, layers, unroll, own_rows, owners)
    vmem = pl.BlockSpec(memory_space=pltpu.VMEM)
    dma = pltpu.SemaphoreType.DMA
    emb, grad, loss = pl.pallas_call(
        functools.partial(kernel, sizes),
        out_shape=(
            jax.ShapeDtypeStruct((G * configs, feat), bf16),
            jax.ShapeDtypeStruct((feat, feat), f32),
            jax.ShapeDtypeStruct((1, 1), f32),
        ),
        in_specs=[pl.BlockSpec(memory_space=pl.ANY)] * 8,
        out_specs=(vmem, vmem, vmem),
        scratch_shapes=[pltpu.VMEM((configs, wide, feat), bf16)] * 3
        + [
            pltpu.VMEM((layers, configs, 2 * rim, feat), bf16),
            pltpu.VMEM((G * configs, feat), f32),
            pltpu.VMEM((S, own_rows, feat), f32),
            pltpu.VMEM((Q, G * configs, feat), bf16),
            pltpu.VMEM((Q, G * configs, total), bf16),
            pltpu.VMEM((G, total, total), f32),
            pltpu.VMEM((nodes, wide), bf16),
            pltpu.VMEM((2 * rim, nodes), bf16),
            pltpu.VMEM((16, nodes), bf16),
            pltpu.VMEM((layers, feat, feat), bf16),
            pltpu.VMEM((nodes, LANES), f32),
            pltpu.VMEM((wide, nodes), jnp.int32),
            pltpu.VMEM((2, rim), jnp.int32),
            pltpu.VMEM((1, nodes), jnp.int32),
            pltpu.VMEM((layers, feat, feat), bf16),
            pltpu.VMEM((feat, feat), bf16),
            pltpu.VMEM((G * configs, partners.shape[2]), jnp.int32),
            pltpu.VMEM((G, total), jnp.int32),
            dma((7,)),
            dma((chunks,)),
            dma((layers, 2, chunks)),
            dma((layers, 2, chunks)),
            dma((owners,)),
            dma((S,)),
            dma((S - 1,)),
            dma((owners,)),
            dma((Q - 1, owners)),
            dma((Q - 1, owners)),
            dma((Q - 1,)),
            dma((Q - 1,)),
        ],
        compiler_params=pltpu.CompilerParams(
            collective_id=0, has_side_effects=True, vmem_limit_bytes=63 * 1024 * 1024
        ),
    )(
        node_feats,
        adjacency.T,
        halo_rows.reshape(2, rim),
        node_graph.reshape(1, nodes),
        layer_weights,
        bilinear,
        partners.reshape(G * configs, partners.shape[2]),
        ranking,
    )
    emb, grad = pl.pallas_call(
        hand_over,
        out_shape=(jax.ShapeDtypeStruct(emb.shape, bf16), jax.ShapeDtypeStruct(grad.shape, f32)),
        in_specs=[vmem] * 2,
        out_specs=(vmem, vmem),
        compiler_params=pltpu.CompilerParams(vmem_limit_bytes=63 * 1024 * 1024),
    )(emb, grad)
    return emb.reshape(G, configs, feat), grad, loss.reshape(())


def solution(mesh):
    placed = (
        P("cfg", "seg", None),
        P("seg", None),
        P("seg", None, None),
        P("seg"),
        P(),
        P(),
        P(None, "cfg", None),
        P(),
    )
    return jax.shard_map(
        functools.partial(on_device, mesh.shape["seg"], mesh.shape["cfg"]),
        mesh=mesh,
        in_specs=placed,
        out_specs=(P(None, "cfg", None), P(), P()),
        check_vma=False,
    )
```

```python
import functools

import jax
import jax.numpy as jnp
from jax import lax
from jax.experimental import pallas as pl
from jax.experimental.pallas import tpu as pltpu
from jax.sharding import PartitionSpec as P

P_SIZE = 64
G = 4
LANES = 128
eps = 1e-06
MESH = pl.DeviceIdType.MESH
f32, bf16 = jnp.float32, jnp.bfloat16


def dot(a, b):
    return jnp.dot(a, b, preferred_element_type=f32)


def split3(values):
    high = values.astype(bf16)
    rest = values - high.astype(f32)
    middle = rest.astype(bf16)
    low = (rest - middle.astype(f32)).astype(bf16)
    return high, middle, low


def each(count, fn):
    lax.fori_loop(0, count, lambda i, c: (fn(i), c)[1], 0)


def column(row, size):
    rows = lax.broadcasted_iota(jnp.int32, (size, size), 0)
    lanes = lax.broadcasted_iota(jnp.int32, (size, size), 1)
    return jnp.sum(jnp.where(rows == lanes, jnp.broadcast_to(row, (size, size)), 0.0), axis=1, keepdims=True)


def kernel(
    sizes,
    feats, *rest,
):
    compute(sizes, feats, rest[:7], *rest[7:])


def compute(
    sizes, feats, sources,
    emb_out, grad_out, loss_out,
    ext0, ext1, ext2, outbox, pooled, parts, emb_all, cnt_all, sgn, adj_mat, pick, member, half_w, eps_wide,
    adjacency, halo_rows, node_graph, weights, bilinear, partners, ranking, small_sem,
    in_sem, halo_send, halo_recv, pool_send, pool_recv, seg_send, seg_recv, cfg_send, cfg_recv, cnt_send, cnt_recv,
):
    S, Q, configs, nodes, feat, rim, layers, unroll, own_rows, owners = sizes
    exts = (ext0, ext1, ext2)
    chunks = configs // unroll
    total = Q * configs
    seg, cfg = lax.axis_index("seg"), lax.axis_index("cfg")

    barrier = pltpu.get_barrier_semaphore()

    def greet(axis, me, count):
        def one(k):
            pl.semaphore_signal(barrier, inc=1, device_id={axis: lax.rem(me + k + 1, count)}, device_id_type=MESH)
        each(count - 1, one)

    greet("seg", seg, S)
    greet("cfg", cfg, Q)

    copies = [
        pltpu.make_async_copy(source, target, small_sem.at[n])
        for n, (source, target) in enumerate(
            zip(sources, (adjacency, halo_rows, node_graph, weights, bilinear, partners, ranking))
        )
    ]
    for copy in copies:
        copy.start()

    def load(i):
        return pltpu.make_async_copy(
            feats.at[pl.ds(i * unroll, unroll)],
            ext0.at[pl.ds(i * unroll, unroll), pl.ds(rim, nodes)],
            in_sem.at[i],
        )

    each(chunks, lambda i: load(i).start())

    for copy in copies:
        copy.wait()
    wide = nodes + 2 * rim
    padded = -(-wide // LANES) * LANES
    turned = jnp.concatenate([adjacency[...].astype(f32), jnp.zeros((padded - wide, nodes), f32)], axis=0)
    adj = turned.T[:, :wide]
    degree = jnp.sum(adj, axis=1, keepdims=True)
    rows = lax.broadcasted_iota(jnp.int32, adj.shape, 0)
    lanes = lax.broadcasted_iota(jnp.int32, adj.shape, 1)
    adj_mat[...] = (adj + jnp.where(lanes == rows + rim, 1.0, 0.0)).astype(bf16)
    eps_wide[...] = jnp.broadcast_to(eps * (1.0 + degree) * (1.0 + degree), (nodes, LANES))
    half_w[...] = (weights[...].astype(f32) * 0.5).astype(bf16)
    node_ids = lax.broadcasted_iota(jnp.int32, (rim, nodes), 1).astype(f32)
    for side in range(2):
        wanted = column(halo_rows[side : side + 1, :].astype(f32), rim)
        pick[side * rim : (side + 1) * rim, :] = jnp.where(node_ids == wanted, 1.0, 0.0).astype(bf16)
    graph_ids = lax.broadcasted_iota(jnp.int32, (16, nodes), 0)
    member[...] = jnp.where(graph_ids == jnp.broadcast_to(node_graph[...], (16, nodes)), 1.0, 0.0).astype(bf16)

    @pl.when(seg == 0)
    def _():
        for ext in exts:
            ext[:, 0:rim, :] = jnp.zeros((configs, rim, feat), bf16)

    @pl.when(seg == S - 1)
    def _():
        for ext in exts:
            ext[:, rim + nodes : 2 * rim + nodes, :] = jnp.zeros((configs, rim, feat), bf16)

    pl.semaphore_wait(barrier, S + Q - 2)

    def halo_copy(l, i, side):
        batch = pl.ds(i * unroll, unroll)
        return pltpu.make_async_remote_copy(
            src_ref=outbox.at[l, batch, pl.ds(side * rim, rim)],
            dst_ref=exts[l].at[batch, pl.ds(0 if side else rim + nodes, rim)],
            send_sem=halo_send.at[l, side, i],
            recv_sem=halo_recv.at[l, side, i],
            device_id={"seg": seg + 1 if side else seg - 1},
            device_id_type=MESH,
        )

    def halo_each(l, i, sends, act):
        up, down = seg < S - 1, seg > 0

        @pl.when(down if sends else up)
        def _():
            act(halo_copy(l, i, 0))

        @pl.when(up if sends else down)
        def _():
            act(halo_copy(l, i, 1))

    def first(i):
        load(i).wait()
        ids = [i * unroll + u for u in range(unroll)]
        blocks = [ext0[c, rim : rim + nodes, :] for c in ids]
        picked = [dot(pick[...], block).astype(bf16) for block in blocks]
        for c, rows in zip(ids, picked):
            outbox[0, c] = rows
        halo_each(0, i, True, lambda copy: copy.start())

    each(chunks, first)

    def layer(l, i):
        halo_each(l, i, False, lambda copy: copy.wait_recv())
        ids = [i * unroll + u for u in range(unroll)]
        before = [exts[l][c] for c in ids]
        summed = [dot(adj_mat[...], block) for block in before]
        normed = []
        for values in summed:
            square = jnp.sum(values * values, axis=1, keepdims=True) * (1.0 / feat)
            scale = lax.rsqrt(jnp.broadcast_to(square, eps_wide.shape) + eps_wide[...])
            normed.append((values * jnp.tile(scale, (1, feat // LANES))).astype(bf16))
        halves = dot(jnp.concatenate(normed, axis=0), half_w[l])
        hidden = []
        for u in range(unroll):
            half = halves[u * nodes : (u + 1) * nodes]
            own = before[u][rim : rim + nodes].astype(f32)
            hidden.append((own + (half + half * jnp.tanh(half))).astype(bf16))
        if l < layers - 1:
            picked = [dot(pick[...], values).astype(bf16) for values in hidden]
            for c, values, rows in zip(ids, hidden, picked):
                exts[l + 1][c, rim : rim + nodes, :] = values
                outbox[l + 1, c] = rows
        else:
            sums = [dot(member[...], values) for values in hidden]
            for c, values in zip(ids, sums):
                for g in range(G):
                    pooled[pl.ds(g * configs + c, 1), :] = values[g : g + 1, :]
        if l < layers - 1:
            halo_each(l + 1, i, True, lambda copy: copy.start())

    for l in range(layers - 1):
        each(chunks, functools.partial(layer, l))

    def pool_copy(source, o):
        return pltpu.make_async_remote_copy(
            src_ref=pooled.at[pl.ds(o * own_rows, own_rows)],
            dst_ref=parts.at[source],
            send_sem=pool_send.at[o],
            recv_sem=pool_recv.at[source],
            device_id={"seg": o},
            device_id_type=MESH,
        )

    groups = max(1, configs // own_rows)
    per_group = chunks // groups

    def last_group(p):
        each(per_group, lambda j: layer(layers - 1, p * per_group + j))

        def send(k):
            o = k * groups + p

            @pl.when(o != seg)
            def _():
                pool_copy(seg, o).start()

        each(owners // groups, send)

    each(groups, last_group)

    block = 16 if (G * configs) % 16 == 0 else 8

    def count(r):
        where = pl.ds(pl.multiple_of(r * block, block), block)
        chosen = partners[where, :]
        ids = lax.broadcasted_iota(jnp.int32, (block, total), 1)
        found = jnp.zeros((block, total), f32)
        for k in range(P_SIZE):
            found = found + jnp.where(chosen[:, k : k + 1] == ids, 1.0, 0.0)
        cnt_all[cfg, where, :] = found.astype(bf16)

    each(G * configs // block, count)

    def cnt_copy(d):
        return pltpu.make_async_remote_copy(
            src_ref=cnt_all.at[cfg],
            dst_ref=cnt_all.at[cfg],
            send_sem=cnt_send.at[d],
            recv_sem=cnt_recv.at[d],
            device_id={"cfg": lax.rem(cfg + d + 1, Q)},
            device_id_type=MESH,
        )

    each(Q - 1, lambda d: cnt_copy(d).start())

    for g in range(G):
        theirs = jnp.broadcast_to(ranking[g : g + 1, :].astype(f32), (total, total))
        ahead = theirs - column(ranking[g : g + 1, :].astype(f32), total)
        sgn[g] = jnp.where(ahead > 0.0, 1.0, jnp.where(ahead < 0.0, -1.0, 0.0))

    for l in range(layers):
        each(chunks, lambda i: halo_each(l, i, True, lambda copy: copy.wait_send()))

    def emb_block(q, o):
        return emb_all.at[q, pl.ds(o * own_rows, own_rows)]

    def seg_copy(k, o):
        return pltpu.make_async_remote_copy(
            src_ref=emb_block(cfg, o),
            dst_ref=emb_block(cfg, o),
            send_sem=seg_send.at[k],
            recv_sem=seg_recv.at[o],
            device_id={"seg": lax.rem(seg + k + 1, S)},
            device_id_type=MESH,
        )

    def cfg_copy(d, q, o):
        return pltpu.make_async_remote_copy(
            src_ref=emb_block(q, o),
            dst_ref=emb_block(q, o),
            send_sem=cfg_send.at[d, o],
            recv_sem=cfg_recv.at[d, o],
            device_id={"cfg": lax.rem(cfg + d + 1, Q)},
            device_id_type=MESH,
        )

    @pl.when(seg < owners)
    def _():
        parts[seg] = pooled[pl.ds(pl.multiple_of(seg * own_rows, own_rows), own_rows), :]

        def arrive(k):
            pool_copy(lax.rem(seg + k + 1, S), seg).wait_recv()

        each(S - 1, arrive)
        summed = parts[0]
        for s in range(1, S):
            summed = summed + parts[s]
        square = jnp.sum(summed * summed, axis=1, keepdims=True) * (1.0 / feat)
        mine = pl.ds(pl.multiple_of(seg * own_rows, own_rows), own_rows)
        emb_all[cfg, mine, :] = (summed * lax.rsqrt(square + eps)).astype(bf16)
        each(S - 1, lambda k: seg_copy(k, seg).start())

    def forward(o):
        @pl.when(o != seg)
        def _():
            seg_copy(0, o).wait_recv()

        each(Q - 1, lambda d: cfg_copy(d, cfg, o).start())

    each(owners, forward)

    emb_out[...] = emb_all[cfg]

    def sent(o):
        @pl.when(o != seg)
        def _():
            pool_copy(seg, o).wait_send()

    each(Q - 1, lambda d: cnt_copy(d).wait())

    def arrived(first, last):
        def one(d):
            source = lax.rem(cfg + Q - d - 1, Q)
            each(last - first, lambda k: cfg_copy(d, source, first + k).wait_recv())

        each(Q - 1, one)

    def of_graph(ref, g):
        if configs % 16 == 0:
            rows = ref[:, g * configs : (g + 1) * configs, :]
        else:
            rows = ref[...].astype(f32)[:, g * configs : (g + 1) * configs, :]
        return rows.reshape(total, rows.shape[2]).astype(bf16)

    grad = jnp.zeros((feat, feat), f32)
    loss = jnp.zeros((1, 1), f32)
    paired = (2 * configs) % own_rows == 0
    if not paired:
        arrived(0, owners)
    for g in range(G):
        if paired and g % 2 == 0:
            arrived(g * configs // own_rows, (g + 2) * configs // own_rows)
        emb = of_graph(emb_all, g)
        often = of_graph(cnt_all, g).astype(f32)
        emb_t = emb.astype(f32).T.astype(bf16)
        projected = dot(emb, bilinear[...])
        stacked = dot(jnp.concatenate(split3(projected), axis=0), emb_t)
        scores = stacked[:total] + stacked[total : 2 * total] + stacked[2 * total :]
        sign = sgn[g]
        margin = 1.0 - sign * scores
        decay = jnp.exp(-jnp.abs(margin))
        soft = jnp.maximum(margin, 0.0) + jnp.log1p(decay)
        sigmoid = jnp.where(margin >= 0.0, 1.0, decay) / (1.0 + decay)
        loss = loss + jnp.sum(often * soft, axis=(0, 1), keepdims=True)
        coef = often * (-sign) * sigmoid * (1.0 / (G * P_SIZE))
        stacked = dot(jnp.concatenate(split3(coef), axis=0), emb)
        carried = stacked[:total] + stacked[total : 2 * total] + stacked[2 * total :]
        high, middle, low = split3(carried)
        grad = grad + (dot(emb_t, high) + dot(emb_t, middle) + dot(emb_t, low))
    grad_out[...] = grad
    loss_out[...] = loss * (1.0 / (G * total * P_SIZE))

    def cfg_sent(d):
        each(owners, lambda o: cfg_copy(d, cfg, o).wait_send())

    each(Q - 1, cfg_sent)
    each(owners, sent)

    @pl.when(seg < owners)
    def _():
        each(S - 1, lambda k: seg_copy(k, seg).wait_send())


def hand_over(emb, grad, emb_out, grad_out):
    emb_out[...] = emb[...]
    grad_out[...] = grad[...]


def on_device(S, Q, node_feats, adjacency, halo_rows, node_graph, layer_weights, bilinear, partners, ranking):
    configs, nodes, feat = node_feats.shape
    rim, layers = halo_rows.shape[2], layer_weights.shape[0]
    unroll = 16 if configs % 16 == 0 else 8 if configs % 8 == 0 else 4
    chunks = configs // unroll
    own_rows = max(16, G * configs // S)
    owners = G * configs // own_rows
    total = Q * configs
    wide = nodes + 2 * rim
    sizes = (S, Q, configs, nodes, feat, rim, layers, unroll, own_rows, owners)
    vmem = pl.BlockSpec(memory_space=pltpu.VMEM)
    dma = pltpu.SemaphoreType.DMA
    emb, grad, loss = pl.pallas_call(
        functools.partial(kernel, sizes),
        out_shape=(
            jax.ShapeDtypeStruct((G * configs, feat), bf16),
            jax.ShapeDtypeStruct((feat, feat), f32),
            jax.ShapeDtypeStruct((1, 1), f32),
        ),
        in_specs=[pl.BlockSpec(memory_space=pl.ANY)] * 8,
        out_specs=(vmem, vmem, vmem),
        scratch_shapes=[pltpu.VMEM((configs, wide, feat), bf16)] * 3
        + [
            pltpu.VMEM((layers, configs, 2 * rim, feat), bf16),
            pltpu.VMEM((G * configs, feat), f32),
            pltpu.VMEM((S, own_rows, feat), f32),
            pltpu.VMEM((Q, G * configs, feat), bf16),
            pltpu.VMEM((Q, G * configs, total), bf16),
            pltpu.VMEM((G, total, total), f32),
            pltpu.VMEM((nodes, wide), bf16),
            pltpu.VMEM((2 * rim, nodes), bf16),
            pltpu.VMEM((16, nodes), bf16),
            pltpu.VMEM((layers, feat, feat), bf16),
            pltpu.VMEM((nodes, LANES), f32),
            pltpu.VMEM((wide, nodes), jnp.int32),
            pltpu.VMEM((2, rim), jnp.int32),
            pltpu.VMEM((1, nodes), jnp.int32),
            pltpu.VMEM((layers, feat, feat), bf16),
            pltpu.VMEM((feat, feat), bf16),
            pltpu.VMEM((G * configs, partners.shape[2]), jnp.int32),
            pltpu.VMEM((G, total), jnp.int32),
            dma((7,)),
            dma((chunks,)),
            dma((layers, 2, chunks)),
            dma((layers, 2, chunks)),
            dma((owners,)),
            dma((S,)),
            dma((S - 1,)),
            dma((owners,)),
            dma((Q - 1, owners)),
            dma((Q - 1, owners)),
            dma((Q - 1,)),
            dma((Q - 1,)),
        ],
        compiler_params=pltpu.CompilerParams(
            collective_id=0, has_side_effects=True, vmem_limit_bytes=63 * 1024 * 1024
        ),
    )(
        node_feats,
        adjacency.T,
        halo_rows.reshape(2, rim),
        node_graph.reshape(1, nodes),
        layer_weights,
        bilinear,
        partners.reshape(G * configs, partners.shape[2]),
        ranking,
    )
    emb, grad = pl.pallas_call(
        hand_over,
        out_shape=(jax.ShapeDtypeStruct(emb.shape, bf16), jax.ShapeDtypeStruct(grad.shape, f32)),
        in_specs=[vmem] * 2,
        out_specs=(vmem, vmem),
        compiler_params=pltpu.CompilerParams(vmem_limit_bytes=63 * 1024 * 1024),
    )(emb, grad)
    return emb.reshape(G, configs, feat), grad, loss.reshape(())


def solution(mesh):
    placed = (
        P("cfg", "seg", None),
        P("seg", None),
        P("seg", None, None),
        P("seg"),
        P(),
        P(),
        P(None, "cfg", None),
        P(),
    )
    return jax.shard_map(
        functools.partial(on_device, mesh.shape["seg"], mesh.shape["cfg"]),
        mesh=mesh,
        in_specs=placed,
        out_specs=(P(None, "cfg", None), P(), P()),
        check_vma=False,
    )
```
